768 devices in a mesh: dp: 48 (over z, y_hi, core), tensor: 16 (over x, y_lo).
Axes of the slice: x: 4, y: 8 (y_hi: 2, y_lo: 4; y = y_hi * 4 + y_lo), z: 12, core: 2. Of those that a mesh axis runs over, the one named last changes fastest.
Arguments:
- rows: bfloat16 [192, 128, 5120], P('dp', None, 'tensor'), may hold values from -6 to 6
- counts: int32 [48], replicated, may hold values from 1 to 4, as said below
- partner: int32 [48], replicated, may hold values from 0 to 47, as said below
- w_kv: bfloat16 [5120, 2048], P('tensor'), may hold values from -0.078125 to 0.078125
- k_gain: float32 [128], replicated, may hold values from 0.1 to 1.9
- cotangent: bfloat16 [144, 128, 2048], P('dp', None, 'tensor'), may hold values from -6 to 6
Outputs:
- keys_values: float32 [144, 128, 2048], P('dp', None, 'tensor')
- rows_grad: float32 [144, 128, 5120], P('dp', None, 'tensor')
- weight_grad: float32 [5120, 2048], P('tensor')
- gain_grad: float32 [128], replicated
The draws below stay inside these ranges and needn't reach their ends.
Inputs may be any that keep to these rules, and one draw needn't show every extreme that they name: `counts`: half of the data indices have one live row; each of the others has 2 to 4, and some index has 4. partner pairs the data indices in two: partner[partner[d]] = d and partner[d] != d; every index with more than one live row is paired with an index with one live row, and among those the ones with more rows are paired with the ones earlier in an order fixed by the draw. Some index with 4 rows is paired with the index after it (counted round). After balancing some index has 3 live rows.
All inputs are finite; a program needn't handle non-finite values.
Results may differ from the reference program's by a relative error of at most 0.0024.
Values may be sent and summed in bfloat16 or wider, within the bound.
A program may use at most 32 MiB of HBM per device.

```python
import jax
import jax.numpy as jnp
from jax import lax

D = 5120
KV = 8
HD = 128
ROW = 128
CAP = 4
BAL = 3
KVW = 2048
SLOTS = 192
BSLOTS = 144
N_DP = 48
N_TENSOR = 16


def pair_loads(key):
    place_key = jax.random.fold_in(key, 101)
    level_key = jax.random.fold_in(key, 202)
    half = N_DP // 2
    rank = jnp.arange(N_DP, dtype=jnp.int32)
    levels = jax.random.randint(level_key, (half,), 2, CAP + 1).astype(jnp.int32)
    levels = levels.at[0].set(CAP)
    levels = jnp.sort(levels)
    rank_counts = jnp.concatenate([jnp.ones((half,), jnp.int32), levels])
    rank_partner = (N_DP - 1 - rank).astype(jnp.int32)
    placed = jax.random.permutation(place_key, N_DP).astype(jnp.int32)
    target = (placed[N_DP - 1] + 1) % N_DP
    holder = jnp.sum(jnp.where(placed == target, rank, 0)).astype(jnp.int32)
    first = placed[0]
    placed = placed.at[holder].set(first)
    placed = placed.at[0].set(target)
    counts = jnp.zeros((N_DP,), jnp.int32).at[placed].set(rank_counts)
    partner = jnp.zeros((N_DP,), jnp.int32).at[placed].set(placed[rank_partner])
    return (counts, partner)


def draw_counts(key, part):
    counts, partner = pair_loads(key)
    return counts


def draw_partner(key, part):
    counts, partner = pair_loads(key)
    return partner


def block_levels(rng, extent, split, smallest, top_value):
    level, own = 1.0, jax.random.fold_in(rng, 6)
    for dim, blocks in split:
        draws = jnp.exp(jax.random.uniform(jax.random.fold_in(own, dim), (blocks,), jnp.float32, smallest / len(split), top_value / len(split)))
        level = level * jnp.repeat(draws, extent[dim] // blocks).reshape([-1 if axis == dim else 1 for axis in range(len(extent))])
    return level


def scatter_about(rng, shape, scale, most, shards=(), held_as=jnp.bfloat16):
    drawn = jax.random.normal(rng, shape, jnp.float32) * scale
    if len(shards) > 0:
        drawn = block_levels(rng, shape, shards, -0.22, 0.18) * drawn
    return jnp.clip(drawn, min=-most, max=most).astype(held_as)


def setup_inputs(seed: int = 0) -> dict:
    arg_keys = jax.random.split(jax.random.key(seed), 7)
    rows = scatter_about(arg_keys[0], (SLOTS, ROW, D), 1.0, 6.0, ((0, 48), (2, 16)))
    counts = draw_counts(jax.random.fold_in(arg_keys[6], 71), 0)
    partner = draw_partner(jax.random.fold_in(arg_keys[6], 71), 0)
    w_kv = scatter_about(arg_keys[3], (D, KVW), D ** -0.5, 0.078125, ((0, 16),))
    k_gain = jnp.clip(1.0 + 0.18 * jax.random.normal(arg_keys[4], (HD,), jnp.float32), 0.1, 1.9)
    cotangent = scatter_about(arg_keys[5], (BSLOTS, ROW, KVW), 1.0, 6.0, ((0, 48), (2, 16)))
    return dict(rows=rows, counts=counts, partner=partner, w_kv=w_kv, k_gain=k_gain, cotangent=cotangent)


def reference(rows, counts, partner, w_kv, k_gain, cotangent):
    theirs = counts[partner]
    out_rows = jnp.maximum(counts - theirs, 0) // 2
    in_rows = jnp.maximum(theirs - counts, 0) // 2
    keep = counts - out_rows
    new_count = keep + in_rows
    slot = jnp.arange(BAL, dtype=jnp.int32)[None, :]
    index = jnp.arange(N_DP, dtype=jnp.int32)[:, None]
    own_source = index * CAP + slot
    in_source = partner[:, None] * CAP + (theirs - in_rows)[:, None] + (slot - keep[:, None])
    source = jnp.where(slot < keep[:, None], own_source, in_source)
    live = slot < new_count[:, None]
    source = jnp.where(live, source, 0).reshape(-1).astype(jnp.int32)
    live_flat = live.reshape(-1)
    taken = rows[source]
    balanced = jnp.where(live_flat[:, None, None], taken, jnp.zeros_like(taken))
    flat = balanced.reshape(N_DP * BAL * ROW, D)
    block = D // N_TENSOR
    flat_blocks = flat.reshape(N_DP * BAL * ROW, N_TENSOR, block)
    weight_blocks = w_kv.reshape(N_TENSOR, block, KVW)

    def add_block(total, shard):
        piece = lax.dynamic_index_in_dim(flat_blocks, shard, 1, keepdims=False)
        wpiece = lax.dynamic_index_in_dim(weight_blocks, shard, 0, keepdims=False)
        part = jnp.dot(piece, wpiece, preferred_element_type=jnp.float32)
        return (total + part, None)
    kv, _ = lax.scan(add_block, jnp.zeros((N_DP * BAL * ROW, KVW), jnp.float32), jnp.arange(N_TENSOR, dtype=jnp.int32))
    heads = kv.reshape(-1, 2 * KV, HD)
    mean_sq = lax.optimization_barrier(jnp.mean(heads * heads, axis=-1, keepdims=True))
    inverse = lax.rsqrt(mean_sq + 1e-06)
    normed = heads * inverse
    is_key = (jnp.arange(2 * KV, dtype=jnp.int32) < KV)[None, :, None]
    token_live = jnp.repeat(live_flat, ROW)[:, None, None]
    result = jnp.where(is_key, normed * k_gain, heads)
    keys_values = jnp.where(token_live, result, 0.0).astype(jnp.float32).reshape(N_DP * BAL, ROW, KVW)
    grad_in = jnp.where(token_live, cotangent.astype(jnp.float32).reshape(-1, 2 * KV, HD), 0.0)
    grad_normed = grad_in * k_gain
    grad_key = inverse * (grad_normed - normed * lax.optimization_barrier(jnp.mean(grad_normed * normed, axis=-1, keepdims=True)))
    grad_kv = jnp.where(is_key, grad_key, grad_in).astype(jnp.bfloat16).reshape(-1, KVW)
    scale = lax.rsqrt((jnp.sum(counts) * ROW).astype(jnp.float32))
    gain_grad = lax.optimization_barrier(jnp.sum(jnp.where(is_key, grad_in * normed, 0.0), axis=(0, 1))) * scale
    rows_grad = jnp.dot(grad_kv, w_kv.T, preferred_element_type=jnp.float32).reshape(N_DP * BAL, ROW, D)
    weight_grad = jnp.dot(flat.T, grad_kv, preferred_element_type=jnp.float32) * scale
    return (keys_values, rows_grad, weight_grad, gain_grad)
```

```python
import functools

import jax
import jax.numpy as jnp
from jax import lax
from jax.experimental import pallas as pl
from jax.experimental.pallas import tpu as pltpu
from jax.sharding import PartitionSpec as P

MESH = pl.DeviceIdType.MESH
F32 = jnp.float32
BF16 = jnp.bfloat16

KV = 8
HD = 128
ROW = 128
CAP = 4
BAL = 3
NX = 4
NY = 4
NZ = 12
NDP = 48
MIDS = 24
FEAT = 320
WIDE = 2048
GROUP = 512
TILES = 14
BLOCK = 15
HALF_TILES = 160
ORDER = (0, 2, 1)
SUBS = ((0, 8), (8, 7))


def remote(src, dst, send, recv, dp, tensor):
    return pltpu.make_async_remote_copy(
        src_ref=src,
        dst_ref=dst,
        send_sem=send,
        recv_sem=recv,
        device_id=(dp, tensor),
        device_id_type=MESH,
    )


def exchange_kernel(counts, partner, rows, moved, offer, held, picked, send1, recv1, send2, recv2):
    me = lax.axis_index("dp")
    tensor = lax.axis_index("tensor")
    chip = me // 2
    is_mid = (me % 2) == (chip % 2)

    barrier = pltpu.get_barrier_semaphore()

    @pl.loop(1, NDP)
    def _(k):
        pl.semaphore_signal(barrier, inc=1, device_id=(lax.rem(me + k, NDP), tensor), device_id_type=MESH)

    last = jnp.clip(counts[me] - 1, 0, CAP - 1)
    offer[0:8] = rows[last, :, 0:128].reshape(8, 16, 128)
    offer[8:16] = rows[last, :, 128:256].reshape(8, 16, 128)
    tail = rows[last, :, 256:320]
    offer[16:24] = jnp.concatenate([tail, jnp.zeros_like(tail)], axis=1).reshape(8, 16, 128)
    pl.semaphore_wait(barrier, NDP - 1)

    def first(j):
        return remote(offer.at[j], held.at[me], send1.at[j], recv1.at[me], 2 * j + j % 2, tensor)

    @pl.loop(0, MIDS)
    def _(k):
        j = lax.rem(chip + k, MIDS)

        @pl.when(2 * j + j % 2 != me)
        def _():
            first(j).start()

    @pl.when(is_mid)
    def _():
        held[me] = offer[chip]

        @pl.loop(1, NDP)
        def _(k):
            s = lax.rem(me + k, NDP)
            remote(offer.at[0], held.at[s], send1.at[0], recv1.at[s], me, tensor).wait_recv()

        @pl.loop(1, NDP)
        def _(k):
            d = lax.rem(me + k, NDP)
            picked[d] = held[partner[d]]
            remote(picked.at[d], moved.at[chip], send2.at[d], recv2.at[chip], d, tensor).start()

        moved[chip] = held[partner[me]]

    @pl.loop(0, MIDS)
    def _(k):
        j = lax.rem(chip + k, MIDS)

        @pl.when(2 * j + j % 2 != me)
        def _():
            remote(picked.at[0], moved.at[j], send2.at[0], recv2.at[j], me, tensor).wait_recv()
            first(j).wait_send()

    @pl.when(is_mid)
    def _():
        @pl.loop(1, NDP)
        def _(k):
            d = lax.rem(me + k, NDP)
            remote(picked.at[d], moved.at[chip], send2.at[d], recv2.at[chip], d, tensor).wait_send()


def exchange(counts, partner, rows):
    vmem = pl.BlockSpec(memory_space=pltpu.VMEM)
    smem = pl.BlockSpec(memory_space=pltpu.SMEM)
    dma = pltpu.SemaphoreType.DMA
    return pl.pallas_call(
        exchange_kernel,
        out_shape=jax.ShapeDtypeStruct((MIDS, 16, 128), BF16),
        in_specs=[smem, smem, vmem],
        out_specs=vmem,
        scratch_shapes=[
            pltpu.VMEM((MIDS, 16, 128), BF16),
            pltpu.VMEM((NDP, 16, 128), BF16),
            pltpu.VMEM((NDP, 16, 128), BF16),
            dma((MIDS,)),
            dma((NDP,)),
            dma((NDP,)),
            dma((MIDS,)),
        ],
        compiler_params=pltpu.CompilerParams(
            collective_id=0, has_side_effects=True, vmem_limit_bytes=16 * 1024 * 1024
        ),
        name="row_exchange",
    )(counts, partner, rows)


def segments(head):
    out, at = [], head * 20
    end = at + 20
    while at < end:
        stop = min(end, (at // TILES + 1) * TILES)
        out.append((at, stop, (at // TILES) * BLOCK + at % TILES))
        at = stop
    return out


def main_kernel(
    counts, partner, rows, moved, w, k_gain, cot,
    kv_out, rg_out, wg_out, gain_out,
    x_all, x_t, sx, rx, acc, sy, ry, dkv, gain_all, w_away, w_core, w_own, ring_m, ring_p, y_in, ag, ag_mate,
    sx_s, rx_s, sy_s, ry_s, day_s, day_r, dax_s, dax_r, gy_s, gy_r, gx_s, gx_r,
    core_s, core_r, zm_s, zm_r, zp_s, zp_r, yh_s, yh_r, am_s, am_r, ap_s, ap_r, mate_s, mate_r,
):
    dp = lax.axis_index("dp")
    t = lax.axis_index("tensor")
    z, yh, core = dp // 4, (dp // 2) % 2, dp % 2
    x, y = t // NY, t % NY

    def dp_at(zz, hh, cc):
        return (zz * 2 + hh) * 2 + cc

    mate = dp_at(z, yh, 1 - core)
    other_y = dp_at(z, 1 - yh, core)
    up = dp_at(lax.rem(z + 1, NZ), yh, core)
    down = dp_at(lax.rem(z + NZ - 1, NZ), yh, core)

    def x_mate(k):
        return lax.rem(x + k, NX) * NY + y

    def y_mate(k):
        return x * NY + lax.rem(y + k, NY)

    barrier = pltpu.get_barrier_semaphore()
    for who in (mate, other_y, up, down):
        pl.semaphore_signal(barrier, inc=1, device_id=(who, t), device_id_type=MESH)
    for k in (1, 2, 3):
        pl.semaphore_signal(barrier, inc=1, device_id=(dp, x_mate(k)), device_id_type=MESH)
        pl.semaphore_signal(barrier, inc=1, device_id=(dp, y_mate(k)), device_id_type=MESH)

    mine = counts[dp]
    theirs = counts[partner[dp]]
    out_rows = jnp.maximum(mine - theirs, 0) // 2
    in_rows = jnp.maximum(theirs - mine, 0) // 2
    keep = mine - out_rows
    new_count = keep + in_rows

    def columns(at, size):
        return pl.ds(pl.multiple_of(at, 128), size)

    pending = []

    def go(copy):
        copy.start()
        pending.append(copy)
        return copy

    arrive_x = {}
    for n, s in enumerate(ORDER):
        own = rows[s]
        came = jnp.concatenate(
            [moved[0:8].reshape(ROW, 128), moved[8:16].reshape(ROW, 128), moved[16:24].reshape(ROW, 128)[:, :64]],
            axis=1,
        )
        own = jnp.where(s < keep, own, jnp.where(s < new_count, came, jnp.zeros_like(came)))
        x_all[s] = own
        if n == 0:
            pl.semaphore_wait(barrier, 10)
        for k in (2, 1, 3):
            to = lax.rem(x + k, NX)
            sx[s, k - 1] = jnp.dot(own, w[:, columns(to * GROUP, GROUP)], preferred_element_type=F32).astype(BF16)
            arrive_x[s, k] = go(
                remote(sx.at[s, k - 1], rx.at[s, k - 1], sx_s.at[s, k - 1], rx_s.at[s, k - 1], dp, x_mate(k))
            )
        acc[s] = jnp.dot(own, w[:, columns(x * GROUP, GROUP)], preferred_element_type=F32)

    x_t[...] = jnp.concatenate([x_all[0], x_all[1], x_all[2]], axis=0).T

    arrive_y = {}
    for s in ORDER:
        for k in (2, 1, 3):
            arrive_x[s, k].wait_recv()
        acc[s] = acc[s] + rx[s, 0].astype(F32) + rx[s, 1].astype(F32) + rx[s, 2].astype(F32)
        for k in (2, 1, 3):
            to = lax.rem(y + k, NY)
            sy[s, k - 1] = acc[s, :, columns(to * HD, HD)].astype(BF16)
            arrive_y[s, k] = go(
                remote(sy.at[s, k - 1], ry.at[s, k - 1], sy_s.at[s, k - 1], ry_s.at[s, k - 1], dp, y_mate(k))
            )

    is_key = t < KV
    gain = k_gain[...]
    gain_sum = jnp.zeros((8, HD), F32)
    arrive_dy = {}
    for s in ORDER:
        for k in (2, 1, 3):
            arrive_y[s, k].wait_recv()
        kv = acc[s, :, columns(y * HD, HD)] + ry[s, 0].astype(F32) + ry[s, 1].astype(F32) + ry[s, 2].astype(F32)
        live = s < new_count
        inverse = lax.rsqrt(jnp.mean(kv * kv, axis=-1, keepdims=True) + 1e-06)
        normed = kv * inverse
        kv_out[s] = jnp.where(live, jnp.where(is_key, normed * gain, kv), 0.0)
        g = jnp.where(live, cot[s].astype(F32), 0.0)
        gn = g * gain
        grad_key = inverse * (gn - normed * jnp.mean(gn * normed, axis=-1, keepdims=True))
        here = (pl.ds(s * ROW, ROW), columns(t * HD, HD))
        dkv[here] = jnp.where(is_key, grad_key, g).astype(BF16)
        for k in (2, 1, 3):
            arrive_dy[s, k] = go(
                remote(dkv.at[here], dkv.at[here], day_s.at[s, k - 1], day_r.at[s, k - 1], dp, y_mate(k))
            )
        gain_sum = gain_sum + jnp.sum((g * normed).reshape(ROW // 8, 8, HD), axis=0)
    gain_all[t] = jnp.where(is_key, gain_sum, 0.0)
    arrive_gy = {}
    for k in (2, 1, 3):
        arrive_gy[k] = go(remote(gain_all.at[t], gain_all.at[t], gy_s.at[k - 1], gy_r.at[k - 1], dp, y_mate(k)))

    arrive_dx = {}
    for s in ORDER:
        for k in (2, 1, 3):
            arrive_dy[s, k].wait_recv()
        here = (pl.ds(s * ROW, ROW), columns(x * GROUP, GROUP))
        for k in (2, 1, 3):
            arrive_dx[s, k] = go(
                remote(dkv.at[here], dkv.at[here], dax_s.at[s, k - 1], dax_r.at[s, k - 1], dp, x_mate(k))
            )
    arrive_gx = {}
    for k in (2, 1, 3):
        arrive_gy[k].wait_recv()
    for k in (2, 1, 3):
        here = pl.ds(x * NY, NY)
        arrive_gx[k] = go(remote(gain_all.at[here], gain_all.at[here], gx_s.at[k - 1], gx_r.at[k - 1], dp, x_mate(k)))

    for s in ORDER:
        for k in (2, 1, 3):
            arrive_dx[s, k].wait_recv()
    for k in (2, 1, 3):
        arrive_gx[k].wait_recv()

    gain_tile = jnp.concatenate([jnp.sum(gain_all[...], axis=0), jnp.zeros((8, HD), F32)], axis=0)

    def product(half, buffer, each):
        for b in range(12):
            buffer[b * BLOCK + TILES] = gain_tile
        buffer[11 * BLOCK + 6 : 11 * BLOCK + TILES] = jnp.zeros((8, 16, HD), F32)
        for q in range(2):
            value = jnp.dot(x_t[...], dkv[:, columns(half * 1024 + q * GROUP, GROUP)], preferred_element_type=F32)
            for h in range(4):
                head = q * 4 + h
                for at, stop, to in segments(head):
                    lo, hi = (at - head * 20) * 16, (stop - head * 20) * 16
                    buffer[to : to + stop - at] = value[lo:hi, h * HD : (h + 1) * HD].reshape(stop - at, 16, HD)
            each(q)

    cuts = ((0, 5 * BLOCK), (5 * BLOCK, 7 * BLOCK))
    arrive_core = []

    def send_half(q):
        at = pl.ds(*cuts[q])
        arrive_core.append(go(remote(w_away.at[at], w_core.at[at], core_s.at[q], core_r.at[q], mate, t)))

    product(1 - core, w_away, send_half)
    product(core, w_own, lambda q: None)
    for q in range(2):
        arrive_core[q].wait_recv()
        at = pl.ds(*cuts[q])
        w_own[at] = w_own[at] + w_core[at]

    def own_block(target, sub):
        return pl.ds(lax.rem(target + 2 * NZ, NZ) * BLOCK + sub[0], sub[1])

    arrive_m, arrive_p = {}, {}
    for k in range(1, 7):
        for u, sub in enumerate(SUBS):
            part = pl.ds(sub[0], sub[1])
            at = own_block(z - (7 - k), sub)
            if k == 1:
                src = w_own.at[at]
            else:
                arrive_m[k - 1, u].wait_recv()
                ring_m[k - 2, part] = ring_m[k - 2, part] + w_own[at]
                src = ring_m.at[k - 2, part]
            arrive_m[k, u] = go(
                remote(src, ring_m.at[k - 1, part], zm_s.at[k - 1, u], zm_r.at[k - 1, u], down, t)
            )
            if k > 5:
                continue
            at = own_block(z + (6 - k), sub)
            if k == 1:
                src = w_own.at[at]
            else:
                arrive_p[k - 1, u].wait_recv()
                ring_p[k - 2, part] = ring_p[k - 2, part] + w_own[at]
                src = ring_p.at[k - 2, part]
            arrive_p[k, u] = go(
                remote(src, ring_p.at[k - 1, part], zp_s.at[k - 1, u], zp_r.at[k - 1, u], up, t)
            )
        if k <= BAL:
            s = ORDER[k - 1]
            rg_out[s] = lax.dot_general(
                dkv[s * ROW : (s + 1) * ROW, :], w[...], (((1,), (1,)), ((), ())), preferred_element_type=F32
            )
    for u, sub in enumerate(SUBS):
        arrive_p[5, u].wait_recv()
        arrive_m[6, u].wait_recv()
    ring_p[4] = ring_p[4] + ring_m[5] + w_own[own_block(z, (0, BLOCK))]
    swap = go(remote(ring_p.at[4], y_in, yh_s, yh_r, other_y, t))
    swap.wait_recv()
    total = ring_p[4] + y_in[...]
    ag[pl.ds(z * TILES, TILES)] = total[:TILES].astype(BF16)
    gain_out[...] = jnp.sum(total[TILES, :8, :], axis=0, keepdims=True)

    def block(origin):
        return pl.ds(lax.rem(origin + 2 * NZ, NZ) * TILES, TILES)

    arrive_mate = []

    def to_mate(origin, n):
        at = block(origin)
        arrive_mate.append(go(remote(ag.at[at], ag_mate.at[at], mate_s.at[n], mate_r.at[n], mate, t)))

    arrive_m, arrive_p = {}, {}
    for k in range(1, 8):
        if k > 1:
            arrive_m[k - 1].wait_recv()
        if k <= 6:
            at = block(z + k - 1)
            arrive_m[k] = go(remote(ag.at[at], ag.at[at], am_s.at[k - 1], am_r.at[k - 1], down, t))
        if 1 < k <= 6:
            arrive_p[k - 1].wait_recv()
        if k <= 5:
            at = block(z - k + 1)
            arrive_p[k] = go(remote(ag.at[at], ag.at[at], ap_s.at[k - 1], ap_r.at[k - 1], up, t))
        to_mate(z + k - 1, k - 1)
        if 1 < k <= 6:
            to_mate(z - k + 1, 5 + k)
    for h in range(8):
        wg_out[:, columns(core * 1024 + h * HD, HD)] = ag[h * 20 : h * 20 + 20].reshape(FEAT, HD).astype(F32)
    for copy in arrive_mate:
        copy.wait_recv()
    for h in range(8):
        wg_out[:, columns((1 - core) * 1024 + h * HD, HD)] = ag_mate[h * 20 : h * 20 + 20].reshape(FEAT, HD).astype(F32)
    for copy in pending:
        copy.wait_send()


def main(counts, partner, rows, moved, w, k_gain, cot):
    vmem = pl.BlockSpec(memory_space=pltpu.VMEM)
    smem = pl.BlockSpec(memory_space=pltpu.SMEM)
    dma = pltpu.SemaphoreType.DMA
    V = pltpu.VMEM
    return pl.pallas_call(
        main_kernel,
        out_shape=(
            jax.ShapeDtypeStruct((BAL, ROW, HD), F32),
            jax.ShapeDtypeStruct((BAL, ROW, FEAT), F32),
            jax.ShapeDtypeStruct((FEAT, WIDE), F32),
            jax.ShapeDtypeStruct((1, HD), F32),
        ),
        in_specs=[smem, smem, vmem, vmem, vmem, vmem, vmem],
        out_specs=(vmem,) * 4,
        scratch_shapes=[
            V((BAL, ROW, FEAT), BF16),
            V((FEAT, BAL * ROW), BF16),
            V((BAL, 3, ROW, GROUP), BF16),
            V((BAL, 3, ROW, GROUP), BF16),
            V((BAL, ROW, GROUP), F32),
            V((BAL, 3, ROW, HD), BF16),
            V((BAL, 3, ROW, HD), BF16),
            V((BAL * ROW, WIDE), BF16),
            V((NX * NY, 8, HD), F32),
            V((NZ * BLOCK, 16, HD), F32),
            V((NZ * BLOCK, 16, HD), F32),
            V((NZ * BLOCK, 16, HD), F32),
            V((6, BLOCK, 16, HD), F32),
            V((5, BLOCK, 16, HD), F32),
            V((BLOCK, 16, HD), F32),
            V((NZ * TILES, 16, HD), BF16),
            V((NZ * TILES, 16, HD), BF16),
            dma((BAL, 3)), dma((BAL, 3)), dma((BAL, 3)), dma((BAL, 3)),
            dma((BAL, 3)), dma((BAL, 3)), dma((BAL, 3)), dma((BAL, 3)),
            dma((3,)), dma((3,)), dma((3,)), dma((3,)),
            dma((2,)), dma((2,)),
            dma((6, 2)), dma((6, 2)), dma((5, 2)), dma((5, 2)),
            dma(()), dma(()),
            dma((6,)), dma((6,)), dma((5,)), dma((5,)),
            dma((12,)), dma((12,)),
        ],
        compiler_params=pltpu.CompilerParams(
            collective_id=1, has_side_effects=True, vmem_limit_bytes=48 * 1024 * 1024
        ),
        name="kv_grads",
    )(counts, partner, rows, moved, w, k_gain, cot)


def shards(rows, counts, partner, w_kv, k_gain, cotangent):
    moved = exchange(counts, partner, rows)
    kv, rows_grad, weight_sum, gain_sum = main(
        counts, partner, rows, moved, w_kv, k_gain.reshape(1, HD), cotangent
    )
    scale = lax.rsqrt((jnp.sum(counts) * ROW).astype(F32))
    return kv, rows_grad, weight_sum * scale, gain_sum.reshape(HD) * scale


def solution(mesh):
    placed = (P("dp", None, "tensor"), P(), P(), P("tensor", None), P(), P("dp", None, "tensor"))
    return jax.shard_map(
        shards,
        mesh=mesh,
        in_specs=placed,
        out_specs=(P("dp", None, "tensor"), P("dp", None, "tensor"), P("tensor", None), P()),
        check_vma=False,
    )
```

```python
import functools

import jax
import jax.numpy as jnp
from jax import lax
from jax.experimental import pallas as pl
from jax.experimental.pallas import tpu as pltpu
from jax.sharding import PartitionSpec as P

MESH = pl.DeviceIdType.MESH
F32 = jnp.float32
BF16 = jnp.bfloat16

KV = 8
HD = 128
ROW = 128
CAP = 4
BAL = 3
NX = 4
NY = 4
NZ = 12
NDP = 48
FEAT = 320
WIDE = 2048
GROUP = 512
TILES = 14
BLOCK = 15
HALF_TILES = 160
ORDER = (0, 2, 1)
SUBS = ((0, 7), (7, 8))
MIDS = 10
SPAN = 24


def remote(src, dst, send, recv, dp, tensor):
    return pltpu.make_async_remote_copy(
        src_ref=src,
        dst_ref=dst,
        send_sem=send,
        recv_sem=recv,
        device_id=(dp, tensor),
        device_id_type=MESH,
    )


def segments(head):
    out, at = [], head * 20
    end = at + 20
    while at < end:
        stop = min(end, (at // TILES + 1) * TILES)
        out.append((at, stop, (at // TILES) * BLOCK + at % TILES))
        at = stop
    return out


def main_kernel(
    counts, partner, rows_hbm, w_hbm, k_gain, cot_hbm,
    kv_out, rg_out, ag_out, gain_out,
    rows, w, cot, offer, held, picked, moved, x_t, sx, rx, acc, sy, ry, dkv, gain_all, w_away, w_core, w_own, ring_m, ring_p, y_in,
    sx_s, rx_s, sy_s, ry_s, day_s, day_r, dax_s, dax_r, dfx_s, dfx_r, gy_s, gy_r, gx_s, gx_r,
    load_sem, first_s, first_r, second_s, second_r,
    core_s, core_r, zm_s, zm_r, zp_s, zp_r, yh_s, yh_r, am_s, am_r, ap_s, ap_r, mate_s, mate_r,
):
    dp = lax.axis_index("dp")
    t = lax.axis_index("tensor")
    z, yh, core = dp // 4, (dp // 2) % 2, dp % 2
    x, y = t // NY, t % NY

    def dp_at(zz, hh, cc):
        return (zz * 2 + hh) * 2 + cc

    mate = dp_at(z, yh, 1 - core)
    other_y = dp_at(z, 1 - yh, core)
    up = dp_at(lax.rem(z + 1, NZ), yh, core)
    down = dp_at(lax.rem(z + NZ - 1, NZ), yh, core)
    up_two = dp_at(lax.rem(z + 2, NZ), yh, core)
    down_two = dp_at(lax.rem(z + NZ - 2, NZ), yh, core)

    chip = dp // 2
    my_mid = (chip * MIDS + SPAN - 1) // SPAN

    def mid_at(j):
        return 2 * ((j * SPAN) // MIDS) + j % 2

    is_mid = mid_at(my_mid) == dp

    def x_mate(k):
        return lax.rem(x + k, NX) * NY + y

    def y_mate(k):
        return x * NY + lax.rem(y + k, NY)

    loads = [
        pltpu.make_async_copy(src, dst, load_sem.at[n])
        for n, (src, dst) in enumerate(((rows_hbm, rows), (w_hbm, w), (cot_hbm, cot)))
    ]
    for load in loads:
        load.start()

    barrier = pltpu.get_barrier_semaphore()
    for who in (mate, other_y, up, down, up_two, down_two):
        pl.semaphore_signal(barrier, inc=1, device_id=(who, t), device_id_type=MESH)
    for k in (1, 2, 3):
        pl.semaphore_signal(barrier, inc=1, device_id=(dp, x_mate(k)), device_id_type=MESH)
        pl.semaphore_signal(barrier, inc=1, device_id=(dp, y_mate(k)), device_id_type=MESH)

    for j in range(MIDS):

        @pl.when(dp != mid_at(j))
        def _(j=j):
            pl.semaphore_signal(barrier, inc=1, device_id=(mid_at(j), t), device_id_type=MESH)

    @pl.when(is_mid)
    def _():
        @pl.loop(1, NDP)
        def _(k):
            pl.semaphore_signal(barrier, inc=1, device_id=(lax.rem(dp + k, NDP), t), device_id_type=MESH)

    mine = counts[dp]
    theirs = counts[partner[dp]]
    out_rows = jnp.maximum(mine - theirs, 0) // 2
    in_rows = jnp.maximum(theirs - mine, 0) // 2
    keep = mine - out_rows
    new_count = keep + in_rows

    def columns(at, size):
        return pl.ds(pl.multiple_of(at, 128), size)

    pending = []

    def go(copy):
        copy.start()
        pending.append(copy)
        return copy

    arrive_x, arrive_y = {}, {}

    def send_x(s, own):
        x_t[:, s * ROW : (s + 1) * ROW] = own
        flat = own.T
        for k in (2, 1, 3):
            to = lax.rem(x + k, NX)
            sx[s, k - 1] = jnp.dot(flat, w[:, columns(to * GROUP, GROUP)], preferred_element_type=F32).astype(BF16)
            arrive_x[s, k] = go(
                remote(sx.at[s, k - 1], rx.at[s, k - 1], sx_s.at[s, k - 1], rx_s.at[s, k - 1], dp, x_mate(k))
            )
        acc[s] = jnp.dot(flat, w[:, columns(x * GROUP, GROUP)], preferred_element_type=F32)

    def send_y(s):
        for k in (2, 1, 3):
            arrive_x[s, k].wait_recv()
        acc[s] = acc[s] + rx[s, 0].astype(F32) + rx[s, 1].astype(F32) + rx[s, 2].astype(F32)
        for k in (2, 1, 3):
            to = lax.rem(y + k, NY)
            sy[s, k - 1] = acc[s, :, columns(to * HD, HD)].astype(BF16)
            arrive_y[s, k] = go(
                remote(sy.at[s, k - 1], ry.at[s, k - 1], sy_s.at[s, k - 1], ry_s.at[s, k - 1], dp, y_mate(k))
            )

    def first(j):
        return remote(offer.at[j], held.at[dp], first_s.at[j], first_r.at[dp], mid_at(j), t)

    def second(j, d):
        return remote(picked.at[d], moved.at[j], second_s.at[d], second_r.at[j], d, t)

    loads[0].wait()
    offer[...] = rows[jnp.clip(mine - 1, 0, CAP - 1)].reshape(MIDS, 2, 16, HD)

    @pl.when(is_mid)
    def _():
        pl.semaphore_wait(barrier, 12 + 2 * (MIDS - 1) + NDP - MIDS)

    @pl.when(jnp.logical_not(is_mid))
    def _():
        pl.semaphore_wait(barrier, 12 + MIDS)

    for j in range(MIDS):

        @pl.when(dp != mid_at(j))
        def _(j=j):
            first(j).start()

    loads[1].wait()
    send_x(0, jnp.where(0 < keep, rows[0], jnp.zeros((FEAT, ROW), BF16)))
    send_x(2, jnp.where(2 < keep, rows[2], jnp.zeros((FEAT, ROW), BF16)))

    @pl.when(is_mid)
    def _():
        held[dp] = offer[my_mid]

        @pl.loop(1, NDP)
        def _(k):
            s = lax.rem(dp + k, NDP)
            remote(offer.at[0], held.at[s], first_s.at[0], first_r.at[s], dp, t).wait_recv()

        @pl.loop(1, NDP)
        def _(k):
            d = lax.rem(dp + k, NDP)
            picked[d] = held[partner[d]]
            second(my_mid, d).start()

        moved[my_mid] = held[partner[dp]]

    send_y(0)
    send_y(2)
    for j in range(MIDS):

        @pl.when(dp != mid_at(j))
        def _(j=j):
            second(j, 0).wait_recv()

    came = moved[...].reshape(FEAT, ROW)
    send_x(1, jnp.where(1 < keep, rows[1], jnp.where(1 < new_count, came, jnp.zeros((FEAT, ROW), BF16))))
    send_y(1)
    loads[2].wait()

    is_key = t < KV
    gain = k_gain[...]
    gain_sum = jnp.zeros((8, HD), F32)
    arrive_dy = {}
    for s in ORDER:
        for k in (2, 1, 3):
            arrive_y[s, k].wait_recv()
        kv = acc[s, :, columns(y * HD, HD)] + ry[s, 0].astype(F32) + ry[s, 1].astype(F32) + ry[s, 2].astype(F32)
        live = s < new_count
        inverse = lax.rsqrt(jnp.mean(kv * kv, axis=-1, keepdims=True) + 1e-06)
        normed = kv * inverse
        kv_out[s] = jnp.where(live, jnp.where(is_key, normed * gain, kv), 0.0)
        g = jnp.where(live, cot[s].astype(F32), 0.0)
        gn = g * gain
        grad_key = inverse * (gn - normed * jnp.mean(gn * normed, axis=-1, keepdims=True))
        here = (pl.ds(s * ROW, ROW), columns(t * HD, HD))
        dkv[here] = jnp.where(is_key, grad_key, g).astype(BF16)
        for k in (2, 1, 3):
            arrive_dy[s, k] = go(
                remote(dkv.at[here], dkv.at[here], day_s.at[s, k - 1], day_r.at[s, k - 1], dp, y_mate(k))
            )
        gain_sum = gain_sum + jnp.sum((g * normed).reshape(ROW // 8, 8, HD), axis=0)
    gain_all[t] = jnp.where(is_key, gain_sum, 0.0)
    arrive_gy = {}
    for k in (2, 1, 3):
        arrive_gy[k] = go(remote(gain_all.at[t], gain_all.at[t], gy_s.at[k - 1], gy_r.at[k - 1], dp, y_mate(k)))

    def group_rows(s, at, size, group):
        return (pl.ds(s * ROW + at, size), columns(lax.rem(group, NX) * GROUP, GROUP))

    arrive_near, arrive_far = {}, {}

    def send_near(s):
        for k in (1, 2, 3):
            arrive_dy[s, k].wait_recv()
        here = group_rows(s, 0, ROW, x)
        for k in (1, 3):
            arrive_near[s, k] = go(
                remote(dkv.at[here], dkv.at[here], dax_s.at[s, k - 1], dax_r.at[s, k - 1], dp, x_mate(k))
            )

    def send_far(s):
        for n, k in enumerate((1, 3)):
            arrive_near[s, k].wait_recv()
            here = group_rows(s, 64 * n, 64, x + NX - k)
            arrive_far[s, k] = go(
                remote(dkv.at[here], dkv.at[here], dfx_s.at[s, n], dfx_r.at[s, n], dp, x_mate(k))
            )

    def row_grad(s):
        rg_out[s] = lax.dot_general(
            w[...], dkv[s * ROW : (s + 1) * ROW, :], (((1,), (1,)), ((), ())), preferred_element_type=F32
        )

    send_near(0)
    send_near(2)
    send_far(0)
    send_near(1)
    send_far(2)
    arrive_gx = {}
    for k in (2, 1, 3):
        arrive_gy[k].wait_recv()
    for k in (2, 1, 3):
        here = pl.ds(x * NY, NY)
        arrive_gx[k] = go(remote(gain_all.at[here], gain_all.at[here], gx_s.at[k - 1], gx_r.at[k - 1], dp, x_mate(k)))
    send_far(1)
    for s in ORDER:
        for k in (1, 3):
            arrive_far[s, k].wait_recv()
        if s != ORDER[-1]:
            row_grad(s)
    for k in (2, 1, 3):
        arrive_gx[k].wait_recv()

    gain_tile = jnp.concatenate([jnp.sum(gain_all[...], axis=0), jnp.zeros((8, HD), F32)], axis=0)

    def product(half, buffer, each):
        for b in range(12):
            buffer[b * BLOCK + TILES] = gain_tile
        buffer[11 * BLOCK + 6 : 11 * BLOCK + TILES] = jnp.zeros((8, 16, HD), F32)
        for q in range(2):
            value = jnp.dot(x_t[...], dkv[:, columns(half * 1024 + q * GROUP, GROUP)], preferred_element_type=F32)
            for h in range(4):
                head = q * 4 + h
                for at, stop, to in segments(head):
                    lo, hi = (at - head * 20) * 16, (stop - head * 20) * 16
                    buffer[to : to + stop - at] = value[lo:hi, h * HD : (h + 1) * HD].reshape(stop - at, 16, HD)
            each(q)

    cuts = ((0, 5 * BLOCK), (5 * BLOCK, 7 * BLOCK))
    arrive_core = []

    def send_half(q):
        at = pl.ds(*cuts[q])
        arrive_core.append(go(remote(w_away.at[at], w_core.at[at], core_s.at[q], core_r.at[q], mate, t)))

    product(1 - core, w_away, send_half)
    product(core, w_own, lambda q: None)
    for q in range(2):
        arrive_core[q].wait_recv()
        at = pl.ds(*cuts[q])
        w_own[at] = w_own[at] + w_core[at]

    def own_block(target, sub):
        return pl.ds(lax.rem(target + 2 * NZ, NZ) * BLOCK + sub[0], sub[1])

    ways = {
        -1: (ring_m, zm_s, zm_r, down, down_two),
        1: (ring_p, zp_s, zp_r, up, up_two),
    }
    arrive = {}

    def deep(sign, u):
        return (sign < 0) == (u == 0)

    def pass_on(sign, u, d):
        ring, send_sem, recv_sem, one, two = ways[sign]
        part = pl.ds(*SUBS[u])
        own = own_block(z + sign * d, SUBS[u])
        terms = {5: (6,) if deep(sign, u) else (), 3: (5, 4), 1: (3, 2)}.get(d, ())
        for n in terms:
            arrive[sign, u, n].wait_recv()
        if terms:
            value = w_own[own]
            for n in terms:
                value = value + ring[n - 1, part]
            src = ring.at[terms[0] - 1, part]
            src[...] = value
        else:
            src = w_own.at[own]
        to = two if d in (5, 3) else one
        arrive[sign, u, d] = go(
            remote(src, ring.at[d - 1, part], send_sem.at[d - 1, u], recv_sem.at[d - 1, u], to, t)
        )

    both = ((-1, 0), (1, 0), (-1, 1), (1, 1))
    flat_first = sorted(both, key=lambda way: (deep(*way), way[1]))
    for way in both:
        pass_on(*way, 6 if deep(*way) else 5)
    for way in both:
        pass_on(*way, 4)
    row_grad(ORDER[-1])
    for way in both:
        if deep(*way):
            pass_on(*way, 5)
    for way in both:
        pass_on(*way, 2)
    for way in flat_first:
        pass_on(*way, 3)
    for way in flat_first:
        pass_on(*way, 1)
    swaps = []
    for u, sub in enumerate(SUBS):
        part = pl.ds(*sub)
        for sign in (-1, 1):
            arrive[sign, u, 1].wait_recv()
        ring_m[0, part] = ring_m[0, part] + ring_p[0, part] + w_own[own_block(z, sub)]
        swaps.append(go(remote(ring_m.at[0, part], y_in.at[part], yh_s.at[u], yh_r.at[u], other_y, t)))
    live_rows = lax.fori_loop(0, NDP, lambda d, n: n + counts[d], 0)
    scale = lax.rsqrt(jnp.full((1, HD), live_rows * ROW, jnp.int32).astype(F32))
    ag = ag_out.at[core]

    def block(origin, u):
        return pl.ds(lax.rem(origin + 2 * NZ, NZ) * TILES + 7 * u, 7)

    spread, arrive_mate, seen = {}, [], set()

    def ready(sign, u, d):
        if (sign, u, d) not in seen:
            seen.add((sign, u, d))
            spread[sign, u, d].wait_recv()

    def hand_on(sign, u, d):
        back = (d - 1) // 2 * 2
        if back:
            ready(sign, u, back)
        at = block(z - sign * back, u)
        _, _, _, one, two = ways[sign]
        send_sem, recv_sem = (am_s, am_r) if sign < 0 else (ap_s, ap_r)
        spread[sign, u, d] = go(
            remote(ag.at[at], ag.at[at], send_sem.at[d - 1, u], recv_sem.at[d - 1, u], one if d % 2 else two, t)
        )

    def to_mate(origin):
        at = pl.ds(lax.rem(origin + 2 * NZ, NZ) * TILES, TILES)
        n = len(arrive_mate)
        arrive_mate.append(go(remote(ag.at[at], ag.at[at], mate_s.at[n], mate_r.at[n], mate, t)))

    def settle(d):
        for sign in (-1, 1):
            for u in (0, 1):
                ready(sign, u, d)
            to_mate(z - sign * d)

    for u, sub in enumerate(SUBS):
        swaps[u].wait_recv()
        at = pl.ds(sub[0], 7)
        ag_out[core, block(z, u)] = ((ring_m[0, at] + y_in[at]) * scale).astype(BF16)
        for d in (2, 1):
            for sign in (-1, 1):
                hand_on(sign, u, d)
    to_mate(z)
    gain_out[...] = jnp.sum(ring_m[0, TILES, :8, :] + y_in[TILES, :8, :], axis=0, keepdims=True) * scale
    for d in (4, 3):
        for way in both:
            hand_on(*way, d)
    settle(1)
    settle(2)
    for way in both:
        if deep(*way):
            hand_on(*way, 6)
    for way in both:
        hand_on(*way, 5)
    settle(3)
    settle(4)
    settle(5)
    for way in both:
        if deep(*way):
            ready(*way, 6)
    to_mate(z + 6)
    for copy in arrive_mate:
        copy.wait_recv()
    for j in range(MIDS):

        @pl.when(dp != mid_at(j))
        def _(j=j):
            first(j).wait_send()

    @pl.when(is_mid)
    def _():
        @pl.loop(1, NDP)
        def _(k):
            second(my_mid, lax.rem(dp + k, NDP)).wait_send()

    for copy in pending:
        copy.wait_send()


def finish_kernel(kv, rg, ag, gain, kv_out, rg_out, wg_out, gain_out):
    for h in range(8):
        wg_out[:, h * HD : (h + 1) * HD] = ag[0, h * 20 : h * 20 + 20].reshape(FEAT, HD).astype(F32)

    @pl.when(pl.program_id(0) == 0)
    def _():
        kv_out[...] = kv[...]
        rg_out[...] = rg[...]
        gain_out[...] = gain[...]


def main(counts, partner, rows, w, k_gain, cot):
    vmem = pl.BlockSpec(memory_space=pltpu.VMEM)
    smem = pl.BlockSpec(memory_space=pltpu.SMEM)
    hbm = pl.BlockSpec(memory_space=pl.ANY)
    dma = pltpu.SemaphoreType.DMA
    V = pltpu.VMEM
    kv, rg, ag, gain = pl.pallas_call(
        main_kernel,
        out_shape=(
            jax.ShapeDtypeStruct((BAL, ROW, HD), F32),
            jax.ShapeDtypeStruct((BAL, FEAT, ROW), F32),
            jax.ShapeDtypeStruct((2, NZ * TILES, 16, HD), BF16),
            jax.ShapeDtypeStruct((1, HD), F32),
        ),
        in_specs=[smem, smem, hbm, hbm, vmem, hbm],
        out_specs=(vmem,) * 4,
        scratch_shapes=[
            V((CAP, FEAT, ROW), BF16),
            V((FEAT, WIDE), BF16),
            V((BAL, ROW, HD), BF16),
            V((MIDS, 2, 16, HD), BF16),
            V((NDP, 2, 16, HD), BF16),
            V((NDP, 2, 16, HD), BF16),
            V((MIDS, 2, 16, HD), BF16),
            V((FEAT, BAL * ROW), BF16),
            V((BAL, 3, ROW, GROUP), BF16),
            V((BAL, 3, ROW, GROUP), BF16),
            V((BAL, ROW, GROUP), F32),
            V((BAL, 3, ROW, HD), BF16),
            V((BAL, 3, ROW, HD), BF16),
            V((BAL * ROW, WIDE), BF16),
            V((NX * NY, 8, HD), F32),
            V((NZ * BLOCK, 16, HD), F32),
            V((NZ * BLOCK, 16, HD), F32),
            V((NZ * BLOCK, 16, HD), F32),
            V((6, BLOCK, 16, HD), F32),
            V((6, BLOCK, 16, HD), F32),
            V((BLOCK, 16, HD), F32),
            dma((BAL, 3)), dma((BAL, 3)), dma((BAL, 3)), dma((BAL, 3)),
            dma((BAL, 3)), dma((BAL, 3)), dma((BAL, 3)), dma((BAL, 3)),
            dma((BAL, 2)), dma((BAL, 2)),
            dma((3,)), dma((3,)), dma((3,)), dma((3,)),
            dma((3,)), dma((MIDS,)), dma((NDP,)), dma((NDP,)), dma((MIDS,)),
            dma((2,)), dma((2,)),
            dma((6, 2)), dma((6, 2)), dma((6, 2)), dma((6, 2)),
            dma((2,)), dma((2,)),
            dma((6, 2)), dma((6, 2)), dma((6, 2)), dma((6, 2)),
            dma((12,)), dma((12,)),
        ],
        compiler_params=pltpu.CompilerParams(
            collective_id=0, has_side_effects=True, vmem_limit_bytes=56 * 1024 * 1024
        ),
        name="kv_grads",
    )(counts, partner, rows, w, k_gain, cot)
    return pl.pallas_call(
        finish_kernel,
        grid=(2,),
        out_shape=(
            jax.ShapeDtypeStruct((BAL, ROW, HD), F32),
            jax.ShapeDtypeStruct((BAL, FEAT, ROW), F32),
            jax.ShapeDtypeStruct((FEAT, WIDE), F32),
            jax.ShapeDtypeStruct((1, HD), F32),
        ),
        in_specs=[
            pl.BlockSpec((BAL, ROW, HD), lambda i: (0, 0, 0)),
            pl.BlockSpec((BAL, FEAT, ROW), lambda i: (0, 0, 0)),
            pl.BlockSpec((1, NZ * TILES, 16, HD), lambda i: (i, 0, 0, 0)),
            pl.BlockSpec((1, HD), lambda i: (0, 0)),
        ],
        out_specs=(
            pl.BlockSpec((BAL, ROW, HD), lambda i: (0, 0, 0)),
            pl.BlockSpec((BAL, FEAT, ROW), lambda i: (0, 0, 0)),
            pl.BlockSpec((FEAT, WIDE // 2), lambda i: (0, i)),
            pl.BlockSpec((1, HD), lambda i: (0, 0)),
        ),
        compiler_params=pltpu.CompilerParams(vmem_limit_bytes=56 * 1024 * 1024),
        name="unpack",
    )(kv, rg, ag, gain)


def shards(rows, counts, partner, w_kv, k_gain, cotangent):
    kv, rows_grad, weight_grad, gain_grad = main(
        counts, partner, jnp.swapaxes(rows, 1, 2), w_kv, k_gain.reshape(1, HD), cotangent
    )
    return kv, jnp.swapaxes(rows_grad, 1, 2), weight_grad, gain_grad.reshape(HD)


def solution(mesh):
    placed = (P("dp", None, "tensor"), P(), P(), P("tensor", None), P(), P("dp", None, "tensor"))
    return jax.shard_map(
        shards,
        mesh=mesh,
        in_specs=placed,
        out_specs=(P("dp", None, "tensor"), P("dp", None, "tensor"), P("tensor", None), P()),
        check_vma=False,
    )
```

```python
import functools

import jax
import jax.numpy as jnp
from jax import lax
from jax.experimental import pallas as pl
from jax.experimental.pallas import tpu as pltpu
from jax.sharding import PartitionSpec as P

MESH = pl.DeviceIdType.MESH
F32 = jnp.float32
BF16 = jnp.bfloat16

KV = 8
HD = 128
ROW = 128
CAP = 4
BAL = 3
NX = 4
NY = 4
NZ = 12
NDP = 48
FEAT = 320
WIDE = 2048
GROUP = 512
TILES = 14
BLOCK = 15
HALF_TILES = 160
ORDER = (0, 2, 1)
SUBS = ((0, 7), (7, 8))
MIDS = 10
PLACE = {0: 0, 2: 1, 1: 2}


def remote(src, dst, send, recv, dp, tensor):
    return pltpu.make_async_remote_copy(
        src_ref=src,
        dst_ref=dst,
        send_sem=send,
        recv_sem=recv,
        device_id=(dp, tensor),
        device_id_type=MESH,
    )


def segments(head):
    out, at = [], head * 20
    end = at + 20
    while at < end:
        stop = min(end, (at // TILES + 1) * TILES)
        out.append((at, stop, (at // TILES) * BLOCK + at % TILES))
        at = stop
    return out


def main_kernel(
    counts, partner, rows_hbm, w_hbm, k_gain, cot_hbm,
    kv_out, rg_out, ag_out, gain_out,
    rows, w, cot, offer, held, picked, moved, x_t, sx, rx, acc, sy, ry, dkv, dkv_last, sh, rh, gain_all, w_away, w_core, w_own, ring_m, ring_p, y_in,
    sx_s, rx_s, sy_s, ry_s, hx_s, hx_r, hd_s, hd_r, day_s, day_r, dax_s, dax_r, dfx_s, dfx_r, gy_s, gy_r, gx_s, gx_r,
    load_sem, first_s, first_r, second_s, second_r,
    core_s, core_r, zm_s, zm_r, zp_s, zp_r, yh_s, yh_r, am_s, am_r, ap_s, ap_r, mate_s, mate_r,
):
    dp = lax.axis_index("dp")
    t = lax.axis_index("tensor")
    z, yh, core = dp // 4, (dp // 2) % 2, dp % 2
    x, y = t // NY, t % NY

    def dp_at(zz, hh, cc):
        return (zz * 2 + hh) * 2 + cc

    mate = dp_at(z, yh, 1 - core)
    other_y = dp_at(z, 1 - yh, core)
    up = dp_at(lax.rem(z + 1, NZ), yh, core)
    down = dp_at(lax.rem(z + NZ - 1, NZ), yh, core)
    up_two = dp_at(lax.rem(z + 2, NZ), yh, core)
    down_two = dp_at(lax.rem(z + NZ - 2, NZ), yh, core)

    def mid_at(j, hh):
        return dp_at(j, hh, lax.rem(j, 2))

    is_mid = jnp.logical_and(z < MIDS, core == z % 2)
    column = NDP // 2

    def beside(k):
        n = lax.rem(z * 2 + core + k, column)
        return dp_at(n // 2, yh, n % 2)

    def x_mate(k):
        return lax.rem(x + k, NX) * NY + y

    def y_mate(k):
        return x * NY + lax.rem(y + k, NY)

    loads = [
        pltpu.make_async_copy(src, dst, load_sem.at[n])
        for n, (src, dst) in enumerate(((rows_hbm, rows), (w_hbm, w), (cot_hbm, cot)))
    ]
    for load in loads:
        load.start()

    barrier = pltpu.get_barrier_semaphore()
    for who in (mate, other_y, up, down, up_two, down_two):
        pl.semaphore_signal(barrier, inc=1, device_id=(who, t), device_id_type=MESH)
    for k in (1, 2, 3):
        pl.semaphore_signal(barrier, inc=1, device_id=(dp, x_mate(k)), device_id_type=MESH)
        pl.semaphore_signal(barrier, inc=1, device_id=(dp, y_mate(k)), device_id_type=MESH)

    @pl.loop(0, MIDS)
    def _(j):
        @pl.when(dp != mid_at(j, yh))
        def _():
            pl.semaphore_signal(barrier, inc=1, device_id=(mid_at(j, yh), t), device_id_type=MESH)

    @pl.when(is_mid)
    def _():
        @pl.loop(1, NDP)
        def _(k):
            pl.semaphore_signal(barrier, inc=1, device_id=(lax.rem(dp + k, NDP), t), device_id_type=MESH)

    mine = counts[dp]
    theirs = counts[partner[dp]]
    out_rows = jnp.maximum(mine - theirs, 0) // 2
    in_rows = jnp.maximum(theirs - mine, 0) // 2
    keep = mine - out_rows
    new_count = keep + in_rows

    def columns(at, size):
        return pl.ds(pl.multiple_of(at, 128), size)

    pending = []

    def go(copy):
        copy.start()
        pending.append(copy)
        return copy

    arrive_x, arrive_y = {}, {}

    def send_x(s, own):
        x_t[:, PLACE[s] * ROW : (PLACE[s] + 1) * ROW] = own
        flat = own.T
        for k in (2, 1, 3):
            to = lax.rem(x + k, NX)
            sx[s, k - 1] = jnp.dot(flat, w[:, columns(to * GROUP, GROUP)], preferred_element_type=F32).astype(BF16)
            arrive_x[s, k] = go(
                remote(sx.at[s, k - 1], rx.at[s, k - 1], sx_s.at[s, k - 1], rx_s.at[s, k - 1], dp, x_mate(k))
            )
        acc[s] = jnp.dot(flat, w[:, columns(x * GROUP, GROUP)], preferred_element_type=F32)

    def hop_y(s, k):
        sy[s, k - 1] = acc[s, :, columns(lax.rem(y + k, NY) * HD, HD)].astype(BF16)
        arrive_y[s, k] = go(
            remote(sy.at[s, k - 1], ry.at[s, k - 1], sy_s.at[s, k - 1], ry_s.at[s, k - 1], dp, y_mate(k))
        )

    def send_y(s):
        for k in (2, 1, 3):
            arrive_x[s, k].wait_recv()
        acc[s] = acc[s] + rx[s, 0].astype(F32) + rx[s, 1].astype(F32) + rx[s, 2].astype(F32)
        for k in (2, 1, 3):
            hop_y(s, k)

    def send_x_heads(s, own):
        x_t[:, PLACE[s] * ROW : (PLACE[s] + 1) * ROW] = own
        flat = own.T
        for j in (3, 2, 1, 0):
            head = lax.rem(y + j, NY)
            for k in (2, 1, 3):
                at = columns((lax.rem(x + k, NX) * NY + head) * HD, HD)
                sh[j, k - 1] = jnp.dot(flat, w[:, at], preferred_element_type=F32).astype(BF16)
                arrive_x[s, j, k] = go(
                    remote(
                        sh.at[j, k - 1], rh.at[j, k - 1], hx_s.at[j, k - 1], hx_r.at[j, k - 1], dp, x_mate(k)
                    )
                )
        acc[s] = jnp.dot(flat, w[:, columns(x * GROUP, GROUP)], preferred_element_type=F32)

    def send_y_heads(s):
        for j in (3, 2, 1, 0):
            here = columns(lax.rem(y + j, NY) * HD, HD)
            for k in (2, 1, 3):
                arrive_x[s, j, k].wait_recv()
            acc[s, :, here] = (
                acc[s, :, here] + rh[j, 0].astype(F32) + rh[j, 1].astype(F32) + rh[j, 2].astype(F32)
            )
            if j:
                hop_y(s, j)

    def first(j, hh):
        return remote(offer.at[j], held.at[dp], first_s.at[hh, j], first_r.at[dp], mid_at(j, hh), t)

    def second(j, d):
        return remote(picked.at[d], moved.at[j], second_s.at[d], second_r.at[j], d, t)

    def each_mid(act):
        @pl.loop(0, 2 * MIDS)
        def _(n):
            j, hh = n // 2, n % 2

            @pl.when(dp != mid_at(j, hh))
            def _():
                act(j, hh)

    loads[0].wait()
    offer[...] = rows[jnp.clip(mine - 1, 0, CAP - 1)].reshape(MIDS, 2, 16, HD)

    @pl.when(is_mid)
    def _():
        pl.semaphore_wait(barrier, 12 + 2 * MIDS - 1 + column - 1)

    @pl.when(jnp.logical_not(is_mid))
    def _():
        pl.semaphore_wait(barrier, 12 + 2 * MIDS)

    each_mid(lambda j, hh: first(j, hh).start())

    loads[1].wait()
    send_x(0, jnp.where(0 < keep, rows[0], jnp.zeros((FEAT, ROW), BF16)))
    send_x(2, jnp.where(2 < keep, rows[2], jnp.zeros((FEAT, ROW), BF16)))

    @pl.when(is_mid)
    def _():
        held[dp] = offer[z]

        @pl.loop(1, NDP)
        def _(k):
            s = lax.rem(dp + k, NDP)
            remote(offer.at[0], held.at[s], first_s.at[0, 0], first_r.at[s], dp, t).wait_recv()

        @pl.loop(1, column)
        def _(k):
            d = beside(k)
            picked[d] = held[partner[d]]
            second(z, d).start()

        moved[z] = held[partner[dp]]

    is_key = t < KV
    gain = k_gain[...]
    gain_parts = []
    arrive_dy, arrive_dx, arrive_near, arrive_far = {}, {}, {}, {}

    def grads(s):
        return dkv_last if s == ORDER[-1] else dkv.at[PLACE[s] * ROW : (PLACE[s] + 1) * ROW]

    def norm(s):
        for k in (2, 1, 3):
            arrive_y[s, k].wait_recv()
        kv = acc[s, :, columns(y * HD, HD)] + ry[s, 0].astype(F32) + ry[s, 1].astype(F32) + ry[s, 2].astype(F32)
        live = s < new_count
        inverse = lax.rsqrt(jnp.mean(kv * kv, axis=-1, keepdims=True) + 1e-06)
        normed = kv * inverse
        g = jnp.where(live, cot[s].astype(F32), 0.0)
        gn = g * gain
        grad_key = inverse * (gn - normed * jnp.mean(gn * normed, axis=-1, keepdims=True))
        here = grads(s).at[:, columns(t * HD, HD)]
        here[...] = jnp.where(is_key, grad_key, g).astype(BF16)
        for k in (2, 3, 1):
            arrive_dy[s, k] = go(
                remote(here, here, day_s.at[s, k - 1], day_r.at[s, k - 1], dp, y_mate(k))
            )
        if s == ORDER[-1]:
            send_head(s, 0)
        kv_out[s] = jnp.where(live, jnp.where(is_key, normed * gain, kv), 0.0)
        gain_parts.append(jnp.sum((g * normed).reshape(ROW // 8, 8, HD), axis=0))

    def send_head(s, back):
        here = grads(s).at[:, columns((x * NY + lax.rem(y + NY - back, NY)) * HD, HD)]
        for k in (2, 1, 3):
            arrive_dx[back, k] = go(
                remote(here, here, hd_s.at[back, k - 1], hd_r.at[back, k - 1], dp, x_mate(k))
            )

    def group_rows(s, at, size, group):
        return (pl.ds(PLACE[s] * ROW + at, size), columns(lax.rem(group, NX) * GROUP, GROUP))

    def send_near(s):
        for k in (1, 3, 2):
            arrive_dy[s, k].wait_recv()
        here = group_rows(s, 0, ROW, x)
        for k in (1, 3):
            arrive_near[s, k] = go(
                remote(dkv.at[here], dkv.at[here], dax_s.at[s, k - 1], dax_r.at[s, k - 1], dp, x_mate(k))
            )

    def send_far(s):
        for n, k in enumerate((1, 3)):
            arrive_near[s, k].wait_recv()
            here = group_rows(s, 64 * n, 64, x + NX - k)
            arrive_far[s, k] = go(
                remote(dkv.at[here], dkv.at[here], dfx_s.at[s, n], dfx_r.at[s, n], dp, x_mate(k))
            )

    def row_grad(s):
        for k in (1, 3):
            if (s, k) in arrive_far:
                arrive_far[s, k].wait_recv()
        rg_out[s] = lax.dot_general(
            w[...], grads(s)[...], (((1,), (1,)), ((), ())), preferred_element_type=F32
        )

    send_y(0)
    send_y(2)
    loads[2].wait()
    norm(0)

    @pl.loop(0, MIDS)
    def _(j):
        @pl.when(dp != mid_at(j, yh))
        def _():
            second(j, dp).wait_recv()

    came = moved[...].reshape(FEAT, ROW)
    send_x_heads(1, jnp.where(1 < keep, rows[1], jnp.where(1 < new_count, came, jnp.zeros((FEAT, ROW), BF16))))
    norm(2)
    send_near(0)
    send_near(2)
    send_y_heads(1)
    send_far(0)
    send_far(2)
    norm(1)
    gain_all[t] = jnp.where(is_key, gain_parts[0] + gain_parts[1] + gain_parts[2], 0.0)
    arrive_gy, arrive_gx = {}, {}
    for k in (2, 1, 3):
        arrive_gy[k] = go(remote(gain_all.at[t], gain_all.at[t], gy_s.at[k - 1], gy_r.at[k - 1], dp, y_mate(k)))
    row_grad(0)
    for k in (1, 3, 2):
        arrive_dy[1, k].wait_recv()
        send_head(1, k)
    for k in (1, 3, 2):
        arrive_gy[k].wait_recv()
    for k in (2, 1, 3):
        here = pl.ds(x * NY, NY)
        arrive_gx[k] = go(remote(gain_all.at[here], gain_all.at[here], gx_s.at[k - 1], gx_r.at[k - 1], dp, x_mate(k)))
    row_grad(2)

    def product(half, buffer, rows_at, grad, add, each):
        for q in range(2):
            value = jnp.dot(
                x_t[:, rows_at], grad[:, columns(half * 1024 + q * GROUP, GROUP)], preferred_element_type=F32
            )
            for h in range(4):
                head = q * 4 + h
                for at, stop, to in segments(head):
                    lo, hi = (at - head * 20) * 16, (stop - head * 20) * 16
                    tiles = value[lo:hi, h * HD : (h + 1) * HD].reshape(stop - at, 16, HD)
                    buffer[to : to + stop - at] = buffer[to : to + stop - at] + tiles if add else tiles
            each(q)

    early, late = slice(0, 2 * ROW), slice(2 * ROW, 3 * ROW)
    product(1 - core, w_away, early, dkv, False, lambda q: None)
    product(core, w_own, early, dkv, False, lambda q: None)
    for k in (2, 1, 3):
        arrive_gx[k].wait_recv()
    gain_tile = jnp.concatenate([jnp.sum(gain_all[...], axis=0), jnp.zeros((8, HD), F32)], axis=0)
    for buffer in (w_away, w_own):
        for b in range(12):
            buffer[b * BLOCK + TILES] = gain_tile
        buffer[11 * BLOCK + 6 : 11 * BLOCK + TILES] = jnp.zeros((8, 16, HD), F32)
    for back in (0, 1, 3, 2):
        for k in (2, 1, 3):
            arrive_dx[back, k].wait_recv()

    cuts = ((0, 5 * BLOCK), (5 * BLOCK, 7 * BLOCK))
    arrive_core = []

    def send_half(q):
        at = pl.ds(*cuts[q])
        arrive_core.append(go(remote(w_away.at[at], w_core.at[at], core_s.at[q], core_r.at[q], mate, t)))

    product(1 - core, w_away, late, dkv_last, True, send_half)
    product(core, w_own, late, dkv_last, True, lambda q: None)
    for q in range(2):
        arrive_core[q].wait_recv()
        at = pl.ds(*cuts[q])
        w_own[at] = w_own[at] + w_core[at]

    def own_block(target, sub):
        return pl.ds(lax.rem(target + 2 * NZ, NZ) * BLOCK + sub[0], sub[1])

    ways = {
        -1: (ring_m, zm_s, zm_r, down, down_two),
        1: (ring_p, zp_s, zp_r, up, up_two),
    }
    arrive = {}

    def deep(sign, u):
        return (sign < 0) == (u == 0)

    def pass_on(sign, u, d):
        ring, send_sem, recv_sem, one, two = ways[sign]
        part = pl.ds(*SUBS[u])
        own = own_block(z + sign * d, SUBS[u])
        terms = {5: (6,) if deep(sign, u) else (), 3: (5, 4), 1: (3, 2)}.get(d, ())
        for n in terms:
            arrive[sign, u, n].wait_recv()
        if terms:
            value = w_own[own]
            for n in terms:
                value = value + ring[n - 1, part]
            src = ring.at[terms[0] - 1, part]
            src[...] = value
        else:
            src = w_own.at[own]
        to = two if d in (5, 3) else one
        arrive[sign, u, d] = go(
            remote(src, ring.at[d - 1, part], send_sem.at[d - 1, u], recv_sem.at[d - 1, u], to, t)
        )

    both = ((-1, 0), (1, 0), (-1, 1), (1, 1))
    flat_first = sorted(both, key=lambda way: (deep(*way), way[1]))
    for way in both:
        pass_on(*way, 6 if deep(*way) else 5)
    for way in both:
        pass_on(*way, 4)
    row_grad(ORDER[-1])
    for way in both:
        if deep(*way):
            pass_on(*way, 5)
    for way in both:
        pass_on(*way, 2)
    for way in flat_first:
        pass_on(*way, 3)
    for way in flat_first:
        pass_on(*way, 1)
    swaps = []
    for u, sub in enumerate(SUBS):
        part = pl.ds(*sub)
        for sign in (-1, 1):
            arrive[sign, u, 1].wait_recv()
        ring_m[0, part] = ring_m[0, part] + ring_p[0, part] + w_own[own_block(z, sub)]
        swaps.append(go(remote(ring_m.at[0, part], y_in.at[part], yh_s.at[u], yh_r.at[u], other_y, t)))
    live_rows = lax.fori_loop(0, NDP, lambda d, n: n + counts[d], 0)
    scale = lax.rsqrt(jnp.full((1, HD), live_rows * ROW, jnp.int32).astype(F32))
    ag = ag_out.at[core]

    def block(origin, u):
        return pl.ds(lax.rem(origin + 2 * NZ, NZ) * TILES + 7 * u, 7)

    spread, arrive_mate, seen = {}, [], set()

    def ready(sign, u, d):
        if (sign, u, d) not in seen:
            seen.add((sign, u, d))
            spread[sign, u, d].wait_recv()

    def hand_on(sign, u, d):
        back = (d - 1) // 2 * 2
        if back:
            ready(sign, u, back)
        at = block(z - sign * back, u)
        _, _, _, one, two = ways[sign]
        send_sem, recv_sem = (am_s, am_r) if sign < 0 else (ap_s, ap_r)
        spread[sign, u, d] = go(
            remote(ag.at[at], ag.at[at], send_sem.at[d - 1, u], recv_sem.at[d - 1, u], one if d % 2 else two, t)
        )

    def to_mate(origin):
        at = pl.ds(lax.rem(origin + 2 * NZ, NZ) * TILES, TILES)
        n = len(arrive_mate)
        arrive_mate.append(go(remote(ag.at[at], ag.at[at], mate_s.at[n], mate_r.at[n], mate, t)))

    def settle(d):
        for sign in (-1, 1):
            for u in (0, 1):
                ready(sign, u, d)
            to_mate(z - sign * d)

    for u, sub in enumerate(SUBS):
        swaps[u].wait_recv()
        at = pl.ds(sub[0], 7)
        ag_out[core, block(z, u)] = ((ring_m[0, at] + y_in[at]) * scale).astype(BF16)
        for d in (2, 1):
            for sign in (-1, 1):
                hand_on(sign, u, d)
    to_mate(z)
    gain_out[...] = jnp.sum(ring_m[0, TILES, :8, :] + y_in[TILES, :8, :], axis=0, keepdims=True) * scale
    for d in (4, 3):
        for way in both:
            hand_on(*way, d)
    settle(1)
    settle(2)
    for way in both:
        if deep(*way):
            hand_on(*way, 6)
    for way in both:
        hand_on(*way, 5)
    settle(3)
    settle(4)
    settle(5)
    for way in both:
        if deep(*way):
            ready(*way, 6)
    to_mate(z + 6)
    for copy in arrive_mate:
        copy.wait_recv()
    each_mid(lambda j, hh: first(j, hh).wait_send())

    @pl.when(is_mid)
    def _():
        @pl.loop(1, column)
        def _(k):
            second(z, beside(k)).wait_send()

    for copy in pending:
        copy.wait_send()


def finish_kernel(kv, rg, ag, gain, kv_out, rg_out, wg_out, gain_out):
    for h in range(8):
        wg_out[:, h * HD : (h + 1) * HD] = ag[0, h * 20 : h * 20 + 20].reshape(FEAT, HD).astype(F32)

    @pl.when(pl.program_id(0) == 0)
    def _():
        kv_out[...] = kv[...]
        rg_out[...] = rg[...]
        gain_out[...] = gain[...]


def main(counts, partner, rows, w, k_gain, cot):
    vmem = pl.BlockSpec(memory_space=pltpu.VMEM)
    smem = pl.BlockSpec(memory_space=pltpu.SMEM)
    hbm = pl.BlockSpec(memory_space=pl.ANY)
    dma = pltpu.SemaphoreType.DMA
    V = pltpu.VMEM
    kv, rg, ag, gain = pl.pallas_call(
        main_kernel,
        out_shape=(
            jax.ShapeDtypeStruct((BAL, ROW, HD), F32),
            jax.ShapeDtypeStruct((BAL, FEAT, ROW), F32),
            jax.ShapeDtypeStruct((2, NZ * TILES, 16, HD), BF16),
            jax.ShapeDtypeStruct((1, HD), F32),
        ),
        in_specs=[smem, smem, hbm, hbm, vmem, hbm],
        out_specs=(vmem,) * 4,
        scratch_shapes=[
            V((CAP, FEAT, ROW), BF16),
            V((FEAT, WIDE), BF16),
            V((BAL, ROW, HD), BF16),
            V((MIDS, 2, 16, HD), BF16),
            V((NDP, 2, 16, HD), BF16),
            V((NDP, 2, 16, HD), BF16),
            V((MIDS, 2, 16, HD), BF16),
            V((FEAT, BAL * ROW), BF16),
            V((BAL, 3, ROW, GROUP), BF16),
            V((BAL, 3, ROW, GROUP), BF16),
            V((BAL, ROW, GROUP), F32),
            V((BAL, 3, ROW, HD), BF16),
            V((BAL, 3, ROW, HD), BF16),
            V((2 * ROW, WIDE), BF16),
            V((ROW, WIDE), BF16),
            V((4, 3, ROW, HD), BF16),
            V((4, 3, ROW, HD), BF16),
            V((NX * NY, 8, HD), F32),
            V((NZ * BLOCK, 16, HD), F32),
            V((NZ * BLOCK, 16, HD), F32),
            V((NZ * BLOCK, 16, HD), F32),
            V((6, BLOCK, 16, HD), F32),
            V((6, BLOCK, 16, HD), F32),
            V((BLOCK, 16, HD), F32),
            dma((BAL, 3)), dma((BAL, 3)), dma((BAL, 3)), dma((BAL, 3)),
            dma((4, 3)), dma((4, 3)), dma((4, 3)), dma((4, 3)),
            dma((BAL, 3)), dma((BAL, 3)), dma((BAL, 3)), dma((BAL, 3)),
            dma((BAL, 2)), dma((BAL, 2)),
            dma((3,)), dma((3,)), dma((3,)), dma((3,)),
            dma((3,)), dma((2, MIDS)), dma((NDP,)), dma((NDP,)), dma((MIDS,)),
            dma((2,)), dma((2,)),
            dma((6, 2)), dma((6, 2)), dma((6, 2)), dma((6, 2)),
            dma((2,)), dma((2,)),
            dma((6, 2)), dma((6, 2)), dma((6, 2)), dma((6, 2)),
            dma((12,)), dma((12,)),
        ],
        compiler_params=pltpu.CompilerParams(
            collective_id=0, has_side_effects=True, vmem_limit_bytes=56 * 1024 * 1024
        ),
        name="kv_grads",
    )(counts, partner, rows, w, k_gain, cot)
    return pl.pallas_call(
        finish_kernel,
        grid=(2,),
        out_shape=(
            jax.ShapeDtypeStruct((BAL, ROW, HD), F32),
            jax.ShapeDtypeStruct((BAL, FEAT, ROW), F32),
            jax.ShapeDtypeStruct((FEAT, WIDE), F32),
            jax.ShapeDtypeStruct((1, HD), F32),
        ),
        in_specs=[
            pl.BlockSpec((BAL, ROW, HD), lambda i: (0, 0, 0)),
            pl.BlockSpec((BAL, FEAT, ROW), lambda i: (0, 0, 0)),
            pl.BlockSpec((1, NZ * TILES, 16, HD), lambda i: (i, 0, 0, 0)),
            pl.BlockSpec((1, HD), lambda i: (0, 0)),
        ],
        out_specs=(
            pl.BlockSpec((BAL, ROW, HD), lambda i: (0, 0, 0)),
            pl.BlockSpec((BAL, FEAT, ROW), lambda i: (0, 0, 0)),
            pl.BlockSpec((FEAT, WIDE // 2), lambda i: (0, i)),
            pl.BlockSpec((1, HD), lambda i: (0, 0)),
        ),
        compiler_params=pltpu.CompilerParams(vmem_limit_bytes=56 * 1024 * 1024),
        name="unpack",
    )(kv, rg, ag, gain)


def shards(rows, counts, partner, w_kv, k_gain, cotangent):
    kv, rows_grad, weight_grad, gain_grad = main(
        counts, partner, jnp.swapaxes(rows, 1, 2), w_kv, k_gain.reshape(1, HD), cotangent
    )
    return kv, jnp.swapaxes(rows_grad, 1, 2), weight_grad, gain_grad.reshape(HD)


def solution(mesh):
    placed = (P("dp", None, "tensor"), P(), P(), P("tensor", None), P(), P("dp", None, "tensor"))
    return jax.shard_map(
        shards,
        mesh=mesh,
        in_specs=placed,
        out_specs=(P("dp", None, "tensor"), P("dp", None, "tensor"), P("tensor", None), P()),
        check_vma=False,
    )
```

```python
import functools

import jax
import jax.numpy as jnp
from jax import lax
from jax.experimental import pallas as pl
from jax.experimental.pallas import tpu as pltpu
from jax.sharding import PartitionSpec as P

MESH = pl.DeviceIdType.MESH
F32 = jnp.float32
BF16 = jnp.bfloat16

KV = 8
HD = 128
ROW = 128
CAP = 4
BAL = 3
NX = 4
NY = 4
NZ = 12
NDP = 48
FEAT = 320
WIDE = 2048
GROUP = 512
TILES = 14
BLOCK = 15
HALF_TILES = 160
ORDER = (0, 2, 1)
SUBS = ((0, 7), (7, 8))
MIDS = 10
PLACE = {0: 0, 2: 1, 1: 2}


def remote(src, dst, send, recv, dp, tensor):
    return pltpu.make_async_remote_copy(
        src_ref=src,
        dst_ref=dst,
        send_sem=send,
        recv_sem=recv,
        device_id=(dp, tensor),
        device_id_type=MESH,
    )


def segments(head):
    out, at = [], head * 20
    end = at + 20
    while at < end:
        stop = min(end, (at // TILES + 1) * TILES)
        out.append((at, stop, (at // TILES) * BLOCK + at % TILES))
        at = stop
    return out


def main_kernel(
    counts, partner, rows_hbm, w_hbm, k_gain, cot_hbm,
    kv_out, rg_out, ag_out, gain_out,
    rows, w, cot, offer, held, picked, moved, x_t, sx, rx, acc, sy, ry, dkv, dkv_last, sh, rh, gain_all, w_away, w_core, w_own, ring_m, ring_p, leaf_s, leaf_r, y_in,
    sx_s, rx_s, sy_s, ry_s, hx_s, hx_r, hd_s, hd_r, day_s, day_r, dax_s, dax_r, dfx_s, dfx_r, gy_s, gy_r, gx_s, gx_r,
    load_sem, first_s, first_r, second_s, second_r,
    core_s, core_r, zm_s, zm_r, zp_s, zp_r, yh_s, yh_r, am_s, am_r, ap_s, ap_r, mate_s, mate_r,
):
    dp = lax.axis_index("dp")
    t = lax.axis_index("tensor")
    z, yh, core = dp // 4, (dp // 2) % 2, dp % 2
    x, y = t // NY, t % NY

    def dp_at(zz, hh, cc):
        return (zz * 2 + hh) * 2 + cc

    mate = dp_at(z, yh, 1 - core)
    other_y = dp_at(z, 1 - yh, core)
    up = dp_at(lax.rem(z + 1, NZ), yh, core)
    down = dp_at(lax.rem(z + NZ - 1, NZ), yh, core)
    up_two = dp_at(lax.rem(z + 2, NZ), yh, core)
    down_two = dp_at(lax.rem(z + NZ - 2, NZ), yh, core)

    def mid_at(j, hh):
        return dp_at(j, hh, lax.rem(j, 2))

    is_mid = jnp.logical_and(z < MIDS, core == z % 2)
    column = NDP // 2

    def beside(k):
        n = lax.rem(z * 2 + core + k, column)
        return dp_at(n // 2, yh, n % 2)

    def x_mate(k):
        return lax.rem(x + k, NX) * NY + y

    def y_mate(k):
        return x * NY + lax.rem(y + k, NY)

    loads = [
        pltpu.make_async_copy(src, dst, load_sem.at[n])
        for n, (src, dst) in enumerate(((rows_hbm, rows), (w_hbm, w), (cot_hbm, cot)))
    ]
    for load in loads:
        load.start()

    barrier = pltpu.get_barrier_semaphore()
    for who in (mate, other_y, up, down, up_two, down_two):
        pl.semaphore_signal(barrier, inc=1, device_id=(who, t), device_id_type=MESH)
    for k in (1, 2, 3):
        pl.semaphore_signal(barrier, inc=1, device_id=(dp, x_mate(k)), device_id_type=MESH)
        pl.semaphore_signal(barrier, inc=1, device_id=(dp, y_mate(k)), device_id_type=MESH)

    @pl.loop(0, MIDS)
    def _(j):
        @pl.when(dp != mid_at(j, yh))
        def _():
            pl.semaphore_signal(barrier, inc=1, device_id=(mid_at(j, yh), t), device_id_type=MESH)

    @pl.when(is_mid)
    def _():
        @pl.loop(1, NDP)
        def _(k):
            pl.semaphore_signal(barrier, inc=1, device_id=(lax.rem(dp + k, NDP), t), device_id_type=MESH)

    mine = counts[dp]
    theirs = counts[partner[dp]]
    out_rows = jnp.maximum(mine - theirs, 0) // 2
    in_rows = jnp.maximum(theirs - mine, 0) // 2
    keep = mine - out_rows
    new_count = keep + in_rows

    def columns(at, size):
        return pl.ds(pl.multiple_of(at, 128), size)

    pending = []

    def go(copy):
        copy.start()
        pending.append(copy)
        return copy

    arrive_x, arrive_y = {}, {}

    def send_x(s, own):
        x_t[:, PLACE[s] * ROW : (PLACE[s] + 1) * ROW] = own
        flat = own.T
        for k in (2, 1, 3):
            to = lax.rem(x + k, NX)
            sx[s, k - 1] = jnp.dot(flat, w[:, columns(to * GROUP, GROUP)], preferred_element_type=F32).astype(BF16)
            arrive_x[s, k] = go(
                remote(sx.at[s, k - 1], rx.at[s, k - 1], sx_s.at[s, k - 1], rx_s.at[s, k - 1], dp, x_mate(k))
            )
        acc[s] = jnp.dot(flat, w[:, columns(x * GROUP, GROUP)], preferred_element_type=F32)

    def hop_y(s, k):
        sy[s, k - 1] = acc[s, :, columns(lax.rem(y + k, NY) * HD, HD)].astype(BF16)
        arrive_y[s, k] = go(
            remote(sy.at[s, k - 1], ry.at[s, k - 1], sy_s.at[s, k - 1], ry_s.at[s, k - 1], dp, y_mate(k))
        )

    def send_y(s):
        for k in (2, 1, 3):
            arrive_x[s, k].wait_recv()
        acc[s] = acc[s] + rx[s, 0].astype(F32) + rx[s, 1].astype(F32) + rx[s, 2].astype(F32)
        for k in (2, 1, 3):
            hop_y(s, k)

    def send_x_heads(s, own):
        x_t[:, PLACE[s] * ROW : (PLACE[s] + 1) * ROW] = own
        flat = own.T
        for j in (3, 2, 1, 0):
            head = lax.rem(y + j, NY)
            for k in (2, 1, 3):
                at = columns((lax.rem(x + k, NX) * NY + head) * HD, HD)
                sh[j, k - 1] = jnp.dot(flat, w[:, at], preferred_element_type=F32).astype(BF16)
                arrive_x[s, j, k] = go(
                    remote(
                        sh.at[j, k - 1], rh.at[j, k - 1], hx_s.at[j, k - 1], hx_r.at[j, k - 1], dp, x_mate(k)
                    )
                )
        acc[s] = jnp.dot(flat, w[:, columns(x * GROUP, GROUP)], preferred_element_type=F32)

    def send_y_heads(s):
        for j in (3, 2, 1, 0):
            here = columns(lax.rem(y + j, NY) * HD, HD)
            for k in (2, 1, 3):
                arrive_x[s, j, k].wait_recv()
            acc[s, :, here] = (
                acc[s, :, here] + rh[j, 0].astype(F32) + rh[j, 1].astype(F32) + rh[j, 2].astype(F32)
            )
            if j:
                hop_y(s, j)

    def first(j, hh):
        return remote(offer.at[j], held.at[dp], first_s.at[hh, j], first_r.at[dp], mid_at(j, hh), t)

    def second(j, d):
        return remote(picked.at[d], moved.at[j], second_s.at[d], second_r.at[j], d, t)

    def each_mid(act):
        @pl.loop(0, 2 * MIDS)
        def _(n):
            j, hh = n // 2, n % 2

            @pl.when(dp != mid_at(j, hh))
            def _():
                act(j, hh)

    loads[0].wait()
    offer[...] = rows[jnp.clip(mine - 1, 0, CAP - 1)].reshape(MIDS, 2, 16, HD)

    @pl.when(is_mid)
    def _():
        pl.semaphore_wait(barrier, 12 + 2 * MIDS - 1 + column - 1)

    @pl.when(jnp.logical_not(is_mid))
    def _():
        pl.semaphore_wait(barrier, 12 + 2 * MIDS)

    each_mid(lambda j, hh: first(j, hh).start())

    loads[1].wait()
    send_x(0, jnp.where(0 < keep, rows[0], jnp.zeros((FEAT, ROW), BF16)))

    @pl.when(is_mid)
    def _():
        held[dp] = offer[z]

        @pl.loop(1, NDP)
        def _(k):
            s = lax.rem(dp + k, NDP)
            remote(offer.at[0], held.at[s], first_s.at[0, 0], first_r.at[s], dp, t).wait_recv()

        @pl.loop(1, column)
        def _(k):
            d = beside(k)
            picked[d] = held[partner[d]]
            second(z, d).start()

        moved[z] = held[partner[dp]]

    send_x(2, jnp.where(2 < keep, rows[2], jnp.zeros((FEAT, ROW), BF16)))

    is_key = t < KV
    gain = k_gain[...]
    gain_parts = []
    arrive_dy, arrive_dx, arrive_near, arrive_far = {}, {}, {}, {}

    def grads(s):
        return dkv_last if s == ORDER[-1] else dkv.at[PLACE[s] * ROW : (PLACE[s] + 1) * ROW]

    def norm(s):
        for k in (2, 1, 3):
            arrive_y[s, k].wait_recv()
        kv = acc[s, :, columns(y * HD, HD)] + ry[s, 0].astype(F32) + ry[s, 1].astype(F32) + ry[s, 2].astype(F32)
        live = s < new_count
        inverse = lax.rsqrt(jnp.mean(kv * kv, axis=-1, keepdims=True) + 1e-06)
        normed = kv * inverse
        g = jnp.where(live, cot[s].astype(F32), 0.0)
        gn = g * gain
        grad_key = inverse * (gn - normed * jnp.mean(gn * normed, axis=-1, keepdims=True))
        here = grads(s).at[:, columns(t * HD, HD)]
        here[...] = jnp.where(is_key, grad_key, g).astype(BF16)
        for k in (2, 3, 1):
            arrive_dy[s, k] = go(
                remote(here, here, day_s.at[s, k - 1], day_r.at[s, k - 1], dp, y_mate(k))
            )
        if s == ORDER[-1]:
            send_head(s, 0)
        kv_out[s] = jnp.where(live, jnp.where(is_key, normed * gain, kv), 0.0)
        gain_parts.append(jnp.sum((g * normed).reshape(ROW // 8, 8, HD), axis=0))

    def send_head(s, back):
        here = grads(s).at[:, columns((x * NY + lax.rem(y + NY - back, NY)) * HD, HD)]
        for k in (2, 1, 3):
            arrive_dx[back, k] = go(
                remote(here, here, hd_s.at[back, k - 1], hd_r.at[back, k - 1], dp, x_mate(k))
            )

    def group_rows(s, at, size, group):
        return (pl.ds(PLACE[s] * ROW + at, size), columns(lax.rem(group, NX) * GROUP, GROUP))

    def send_near(s):
        for k in (1, 3, 2):
            arrive_dy[s, k].wait_recv()
        here = group_rows(s, 0, ROW, x)
        for k in (1, 3):
            arrive_near[s, k] = go(
                remote(dkv.at[here], dkv.at[here], dax_s.at[s, k - 1], dax_r.at[s, k - 1], dp, x_mate(k))
            )

    def send_far(s):
        for n, k in enumerate((1, 3)):
            arrive_near[s, k].wait_recv()
            here = group_rows(s, 64 * n, 64, x + NX - k)
            arrive_far[s, k] = go(
                remote(dkv.at[here], dkv.at[here], dfx_s.at[s, n], dfx_r.at[s, n], dp, x_mate(k))
            )

    def row_grad(s):
        for k in (1, 3):
            if (s, k) in arrive_far:
                arrive_far[s, k].wait_recv()
        rg_out[s] = lax.dot_general(
            w[...], grads(s)[...], (((1,), (1,)), ((), ())), preferred_element_type=F32
        )

    send_y(0)
    send_y(2)
    loads[2].wait()
    norm(0)

    @pl.loop(0, MIDS)
    def _(j):
        @pl.when(dp != mid_at(j, yh))
        def _():
            second(j, dp).wait_recv()

    came = moved[...].reshape(FEAT, ROW)
    send_x_heads(1, jnp.where(1 < keep, rows[1], jnp.where(1 < new_count, came, jnp.zeros((FEAT, ROW), BF16))))
    norm(2)
    send_near(0)
    send_near(2)
    send_y_heads(1)
    send_far(0)
    send_far(2)
    norm(1)
    gain_all[t] = jnp.where(is_key, gain_parts[0] + gain_parts[1] + gain_parts[2], 0.0)
    arrive_gy, arrive_gx = {}, {}
    for k in (2, 1, 3):
        arrive_gy[k] = go(remote(gain_all.at[t], gain_all.at[t], gy_s.at[k - 1], gy_r.at[k - 1], dp, y_mate(k)))
    row_grad(0)
    for k in (1, 3, 2):
        arrive_dy[1, k].wait_recv()
        send_head(1, k)
    for k in (1, 3, 2):
        arrive_gy[k].wait_recv()
    for k in (2, 1, 3):
        here = pl.ds(x * NY, NY)
        arrive_gx[k] = go(remote(gain_all.at[here], gain_all.at[here], gx_s.at[k - 1], gx_r.at[k - 1], dp, x_mate(k)))
    row_grad(2)

    def product(half, buffer, rows_at, grad, add, each):
        for q in range(2):
            value = jnp.dot(
                x_t[:, rows_at], grad[:, columns(half * 1024 + q * GROUP, GROUP)], preferred_element_type=F32
            )
            for h in range(4):
                head = q * 4 + h
                for at, stop, to in segments(head):
                    lo, hi = (at - head * 20) * 16, (stop - head * 20) * 16
                    tiles = value[lo:hi, h * HD : (h + 1) * HD].reshape(stop - at, 16, HD)
                    buffer[to : to + stop - at] = buffer[to : to + stop - at] + tiles if add else tiles
            each(q)

    early, late = slice(0, 2 * ROW), slice(2 * ROW, 3 * ROW)
    product(1 - core, w_away, early, dkv, False, lambda q: None)
    product(core, w_own, early, dkv, False, lambda q: None)
    for k in (2, 1, 3):
        arrive_gx[k].wait_recv()
    gain_tile = jnp.concatenate([jnp.sum(gain_all[...], axis=0), jnp.zeros((8, HD), F32)], axis=0)
    for buffer in (w_away, w_own):
        for b in range(12):
            buffer[b * BLOCK + TILES] = gain_tile
        buffer[11 * BLOCK + 6 : 11 * BLOCK + TILES] = jnp.zeros((8, 16, HD), F32)
    for back in (0, 1, 3, 2):
        for k in (2, 1, 3):
            arrive_dx[back, k].wait_recv()

    cuts = ((0, 5 * BLOCK), (5 * BLOCK, 7 * BLOCK))
    arrive_core = []

    def send_half(q):
        at = pl.ds(*cuts[q])
        arrive_core.append(go(remote(w_away.at[at], w_core.at[at], core_s.at[q], core_r.at[q], mate, t)))

    product(1 - core, w_away, late, dkv_last, True, send_half)
    product(core, w_own, late, dkv_last, True, lambda q: None)
    for q in range(2):
        arrive_core[q].wait_recv()
        at = pl.ds(*cuts[q])
        w_own[at] = w_own[at] + w_core[at]

    def own_block(target, sub):
        return pl.ds(lax.rem(target + 2 * NZ, NZ) * BLOCK + sub[0], sub[1])

    ways = {
        -1: (ring_m, zm_s, zm_r, down, down_two),
        1: (ring_p, zp_s, zp_r, up, up_two),
    }
    arrive = {}

    def deep(sign, u):
        return (sign < 0) == (u == 0)

    def ends(sign, u, d):
        return d in (6, 4, 2) or (d == 5 and not deep(sign, u))

    def leaf(sign, d):
        return (0 if sign < 0 else 3) + {6: 0, 5: 0, 4: 1, 2: 2}[d]

    def pass_on(sign, u, d):
        ring, send_sem, recv_sem, one, two = ways[sign]
        part = pl.ds(*SUBS[u])
        own = own_block(z + sign * d, SUBS[u])
        terms = {5: (6,) if deep(sign, u) else (), 3: (5, 4), 1: (3, 2)}.get(d, ())
        for n in terms:
            arrive[sign, u, n].wait_recv()
        value = w_own[own]
        if terms:
            for n in terms:
                value = value + (leaf_r[leaf(sign, n), part].astype(F32) if ends(sign, u, n) else ring[n - 1, part])
            src, dst = ring.at[terms[0] - 1, part], ring.at[d - 1, part]
            src[...] = value
        else:
            at = leaf(sign, d)
            src, dst = leaf_s.at[at, part], leaf_r.at[at, part]
            src[...] = value.astype(BF16)
            if u == 1:
                high = value[7, :8].astype(BF16)
                low = (value[7, :8] - high.astype(F32)).astype(BF16)
                leaf_s[at, TILES] = jnp.concatenate([high, low], axis=0)
        to = two if d in (5, 3) else one
        arrive[sign, u, d] = go(remote(src, dst, send_sem.at[d - 1, u], recv_sem.at[d - 1, u], to, t))

    both = ((-1, 0), (1, 0), (-1, 1), (1, 1))
    flat_first = sorted(both, key=lambda way: (deep(*way), way[1]))
    for way in both:
        pass_on(*way, 6 if deep(*way) else 5)
    for way in both:
        pass_on(*way, 4)
    row_grad(ORDER[-1])
    for way in both:
        if deep(*way):
            pass_on(*way, 5)
    for way in both:
        pass_on(*way, 2)
    for way in flat_first:
        pass_on(*way, 3)
    for way in flat_first:
        pass_on(*way, 1)
    swaps = []
    for u, sub in enumerate(SUBS):
        part = pl.ds(*sub)
        for sign in (-1, 1):
            arrive[sign, u, 1].wait_recv()
        ring_m[0, part] = ring_m[0, part] + ring_p[0, part] + w_own[own_block(z, sub)]
        swaps.append(go(remote(ring_m.at[0, part], y_in.at[part], yh_s.at[u], yh_r.at[u], other_y, t)))
    live_rows = lax.fori_loop(0, NDP, lambda d, n: n + counts[d], 0)
    scale = lax.rsqrt(jnp.full((1, HD), live_rows * ROW, jnp.int32).astype(F32))
    ag = ag_out.at[core]

    def block(origin, u):
        return pl.ds(lax.rem(origin + 2 * NZ, NZ) * TILES + 7 * u, 7)

    spread, arrive_mate, seen = {}, [], set()

    def ready(sign, u, d):
        if (sign, u, d) not in seen:
            seen.add((sign, u, d))
            spread[sign, u, d].wait_recv()

    def hand_on(sign, u, d):
        back = (d - 1) // 2 * 2
        if back:
            ready(sign, u, back)
        at = block(z - sign * back, u)
        _, _, _, one, two = ways[sign]
        send_sem, recv_sem = (am_s, am_r) if sign < 0 else (ap_s, ap_r)
        spread[sign, u, d] = go(
            remote(ag.at[at], ag.at[at], send_sem.at[d - 1, u], recv_sem.at[d - 1, u], one if d % 2 else two, t)
        )

    def to_mate(origin):
        at = pl.ds(lax.rem(origin + 2 * NZ, NZ) * TILES, TILES)
        n = len(arrive_mate)
        arrive_mate.append(go(remote(ag.at[at], ag.at[at], mate_s.at[n], mate_r.at[n], mate, t)))

    def settle(d):
        for sign in (-1, 1):
            for u in (0, 1):
                ready(sign, u, d)
            to_mate(z - sign * d)

    for u, sub in enumerate(SUBS):
        swaps[u].wait_recv()
        at = pl.ds(sub[0], 7)
        ag_out[core, block(z, u)] = ((ring_m[0, at] + y_in[at]) * scale).astype(BF16)
        for d in (2, 1):
            for sign in (-1, 1):
                hand_on(sign, u, d)
    to_mate(z)
    gain_out[...] = jnp.sum(ring_m[0, TILES] + y_in[TILES], axis=0, keepdims=True) * scale
    for d in (4, 3):
        for way in both:
            hand_on(*way, d)
    settle(1)
    settle(2)
    for way in both:
        if deep(*way):
            hand_on(*way, 6)
    for way in both:
        hand_on(*way, 5)
    settle(3)
    settle(4)
    settle(5)
    for way in both:
        if deep(*way):
            ready(*way, 6)
    to_mate(z + 6)
    for copy in arrive_mate:
        copy.wait_recv()
    each_mid(lambda j, hh: first(j, hh).wait_send())

    @pl.when(is_mid)
    def _():
        @pl.loop(1, column)
        def _(k):
            second(z, beside(k)).wait_send()

    for copy in pending:
        copy.wait_send()


def finish_kernel(kv, rg, ag, gain, kv_out, rg_out, wg_out, gain_out):
    for h in range(4):
        wg_out[:, h * HD : (h + 1) * HD] = ag[0, h * 20 : h * 20 + 20].reshape(FEAT, HD).astype(F32)

    @pl.when(pl.program_id(0) == 0)
    def _():
        kv_out[...] = kv[...]
        rg_out[...] = rg[...]
        gain_out[...] = gain[...]


def main(counts, partner, rows, w, k_gain, cot):
    vmem = pl.BlockSpec(memory_space=pltpu.VMEM)
    smem = pl.BlockSpec(memory_space=pltpu.SMEM)
    hbm = pl.BlockSpec(memory_space=pl.ANY)
    dma = pltpu.SemaphoreType.DMA
    V = pltpu.VMEM
    kv, rg, ag, gain = pl.pallas_call(
        main_kernel,
        out_shape=(
            jax.ShapeDtypeStruct((BAL, ROW, HD), F32),
            jax.ShapeDtypeStruct((BAL, FEAT, ROW), F32),
            jax.ShapeDtypeStruct((2, NZ * TILES, 16, HD), BF16),
            jax.ShapeDtypeStruct((1, HD), F32),
        ),
        in_specs=[smem, smem, hbm, hbm, vmem, hbm],
        out_specs=(vmem,) * 4,
        scratch_shapes=[
            V((CAP, FEAT, ROW), BF16),
            V((FEAT, WIDE), BF16),
            V((BAL, ROW, HD), BF16),
            V((MIDS, 2, 16, HD), BF16),
            V((NDP, 2, 16, HD), BF16),
            V((NDP, 2, 16, HD), BF16),
            V((MIDS, 2, 16, HD), BF16),
            V((FEAT, BAL * ROW), BF16),
            V((BAL, 3, ROW, GROUP), BF16),
            V((BAL, 3, ROW, GROUP), BF16),
            V((BAL, ROW, GROUP), F32),
            V((BAL, 3, ROW, HD), BF16),
            V((BAL, 3, ROW, HD), BF16),
            V((2 * ROW, WIDE), BF16),
            V((ROW, WIDE), BF16),
            V((4, 3, ROW, HD), BF16),
            V((4, 3, ROW, HD), BF16),
            V((NX * NY, 8, HD), F32),
            V((NZ * BLOCK, 16, HD), F32),
            V((NZ * BLOCK, 16, HD), F32),
            V((NZ * BLOCK, 16, HD), F32),
            V((6, BLOCK, 16, HD), F32),
            V((6, BLOCK, 16, HD), F32),
            V((6, BLOCK, 16, HD), BF16),
            V((6, BLOCK, 16, HD), BF16),
            V((BLOCK, 16, HD), F32),
            dma((BAL, 3)), dma((BAL, 3)), dma((BAL, 3)), dma((BAL, 3)),
            dma((4, 3)), dma((4, 3)), dma((4, 3)), dma((4, 3)),
            dma((BAL, 3)), dma((BAL, 3)), dma((BAL, 3)), dma((BAL, 3)),
            dma((BAL, 2)), dma((BAL, 2)),
            dma((3,)), dma((3,)), dma((3,)), dma((3,)),
            dma((3,)), dma((2, MIDS)), dma((NDP,)), dma((NDP,)), dma((MIDS,)),
            dma((2,)), dma((2,)),
            dma((6, 2)), dma((6, 2)), dma((6, 2)), dma((6, 2)),
            dma((2,)), dma((2,)),
            dma((6, 2)), dma((6, 2)), dma((6, 2)), dma((6, 2)),
            dma((12,)), dma((12,)),
        ],
        compiler_params=pltpu.CompilerParams(
            collective_id=0, has_side_effects=True, vmem_limit_bytes=56 * 1024 * 1024
        ),
        name="kv_grads",
    )(counts, partner, rows, w, k_gain, cot)
    return pl.pallas_call(
        finish_kernel,
        grid=(4,),
        out_shape=(
            jax.ShapeDtypeStruct((BAL, ROW, HD), F32),
            jax.ShapeDtypeStruct((BAL, FEAT, ROW), F32),
            jax.ShapeDtypeStruct((FEAT, WIDE), F32),
            jax.ShapeDtypeStruct((1, HD), F32),
        ),
        in_specs=[
            pl.BlockSpec((BAL, ROW, HD), lambda i: (0, 0, 0)),
            pl.BlockSpec((BAL, FEAT, ROW), lambda i: (0, 0, 0)),
            pl.BlockSpec((1, HALF_TILES // 2, 16, HD), lambda i: (i // 2, i % 2, 0, 0)),
            pl.BlockSpec((1, HD), lambda i: (0, 0)),
        ],
        out_specs=(
            pl.BlockSpec((BAL, ROW, HD), lambda i: (0, 0, 0)),
            pl.BlockSpec((BAL, FEAT, ROW), lambda i: (0, 0, 0)),
            pl.BlockSpec((FEAT, GROUP), lambda i: (0, i)),
            pl.BlockSpec((1, HD), lambda i: (0, 0)),
        ),
        compiler_params=pltpu.CompilerParams(vmem_limit_bytes=56 * 1024 * 1024),
        name="unpack",
    )(kv, rg, ag, gain)


def shards(rows, counts, partner, w_kv, k_gain, cotangent):
    kv, rows_grad, weight_grad, gain_grad = main(
        counts, partner, jnp.swapaxes(rows, 1, 2), w_kv, k_gain.reshape(1, HD), cotangent
    )
    return kv, jnp.swapaxes(rows_grad, 1, 2), weight_grad, gain_grad.reshape(HD)


def solution(mesh):
    placed = (P("dp", None, "tensor"), P(), P(), P("tensor", None), P(), P("dp", None, "tensor"))
    return jax.shard_map(
        shards,
        mesh=mesh,
        in_specs=placed,
        out_specs=(P("dp", None, "tensor"), P("dp", None, "tensor"), P("tensor", None), P()),
        check_vma=False,
    )
```

```python
import functools

import jax
import jax.numpy as jnp
from jax import lax
from jax.experimental import pallas as pl
from jax.experimental.pallas import tpu as pltpu
from jax.sharding import PartitionSpec as P

MESH = pl.DeviceIdType.MESH
F32 = jnp.float32
BF16 = jnp.bfloat16

KV = 8
HD = 128
ROW = 128
CAP = 4
BAL = 3
NX = 4
NY = 4
NZ = 12
NDP = 48
FEAT = 320
WIDE = 2048
GROUP = 512
TILES = 14
BLOCK = 15
HALF_TILES = 160
ORDER = (0, 2, 1)
SUBS = ((0, 7), (7, 8))
MIDS = 10
PLACE = {0: 0, 2: 1, 1: 2}


def remote(src, dst, send, recv, dp, tensor):
    return pltpu.make_async_remote_copy(
        src_ref=src,
        dst_ref=dst,
        send_sem=send,
        recv_sem=recv,
        device_id=(dp, tensor),
        device_id_type=MESH,
    )


def segments(head):
    out, at = [], head * 20
    end = at + 20
    while at < end:
        stop = min(end, (at // TILES + 1) * TILES)
        out.append((at, stop, (at // TILES) * BLOCK + at % TILES))
        at = stop
    return out


def main_kernel(
    counts, partner, rows_hbm, w_hbm, k_gain, cot_hbm,
    kv_out, rg_out, ag_out, gain_out,
    rows, w, cot, offer, held, picked, moved, x_t, sx, rx, acc, sy, ry, dkv, dkv_last, sh, rh, gain_all, w_away, w_core, w_own, ring_m, ring_p, y_in,
    sx_s, rx_s, sy_s, ry_s, hx_s, hx_r, hd_s, hd_r, day_s, day_r, dax_s, dax_r, dfx_s, dfx_r, gy_s, gy_r, gx_s, gx_r,
    load_sem, first_s, first_r, second_s, second_r,
    core_s, core_r, zm_s, zm_r, zp_s, zp_r, yh_s, yh_r, am_s, am_r, ap_s, ap_r, mate_s, mate_r,
):
    dp = lax.axis_index("dp")
    t = lax.axis_index("tensor")
    z, yh, core = dp // 4, (dp // 2) % 2, dp % 2
    x, y = t // NY, t % NY

    def dp_at(zz, hh, cc):
        return (zz * 2 + hh) * 2 + cc

    mate = dp_at(z, yh, 1 - core)
    other_y = dp_at(z, 1 - yh, core)
    up = dp_at(lax.rem(z + 1, NZ), yh, core)
    down = dp_at(lax.rem(z + NZ - 1, NZ), yh, core)
    up_two = dp_at(lax.rem(z + 2, NZ), yh, core)
    down_two = dp_at(lax.rem(z + NZ - 2, NZ), yh, core)

    def mid_at(j, hh):
        return dp_at(j, hh, lax.rem(j, 2))

    is_mid = jnp.logical_and(z < MIDS, core == z % 2)
    column = NDP // 2

    def beside(k):
        n = lax.rem(z * 2 + core + k, column)
        return dp_at(n // 2, yh, n % 2)

    def x_mate(k):
        return lax.rem(x + k, NX) * NY + y

    def y_mate(k):
        return x * NY + lax.rem(y + k, NY)

    loads = [
        pltpu.make_async_copy(src, dst, load_sem.at[n])
        for n, (src, dst) in enumerate(((rows_hbm, rows), (w_hbm, w), (cot_hbm, cot)))
    ]
    for load in loads:
        load.start()

    barrier = pltpu.get_barrier_semaphore()
    for who in (mate, other_y, up, down, up_two, down_two):
        pl.semaphore_signal(barrier, inc=1, device_id=(who, t), device_id_type=MESH)
    for k in (1, 2, 3):
        pl.semaphore_signal(barrier, inc=1, device_id=(dp, x_mate(k)), device_id_type=MESH)
        pl.semaphore_signal(barrier, inc=1, device_id=(dp, y_mate(k)), device_id_type=MESH)

    @pl.loop(0, MIDS)
    def _(j):
        @pl.when(dp != mid_at(j, yh))
        def _():
            pl.semaphore_signal(barrier, inc=1, device_id=(mid_at(j, yh), t), device_id_type=MESH)

    @pl.when(is_mid)
    def _():
        @pl.loop(1, NDP)
        def _(k):
            pl.semaphore_signal(barrier, inc=1, device_id=(lax.rem(dp + k, NDP), t), device_id_type=MESH)

    mine = counts[dp]
    theirs = counts[partner[dp]]
    out_rows = jnp.maximum(mine - theirs, 0) // 2
    in_rows = jnp.maximum(theirs - mine, 0) // 2
    keep = mine - out_rows
    new_count = keep + in_rows

    def columns(at, size):
        return pl.ds(pl.multiple_of(at, 128), size)

    pending = []

    def go(copy):
        copy.start()
        pending.append(copy)
        return copy

    arrive_x, arrive_y = {}, {}

    def send_x(s, own):
        x_t[:, PLACE[s] * ROW : (PLACE[s] + 1) * ROW] = own
        flat = own.T
        for k in (2, 1, 3):
            to = lax.rem(x + k, NX)
            sx[s, k - 1] = jnp.dot(flat, w[:, columns(to * GROUP, GROUP)], preferred_element_type=F32).astype(BF16)
            arrive_x[s, k] = go(
                remote(sx.at[s, k - 1], rx.at[s, k - 1], sx_s.at[s, k - 1], rx_s.at[s, k - 1], dp, x_mate(k))
            )
        acc[s] = jnp.dot(flat, w[:, columns(x * GROUP, GROUP)], preferred_element_type=F32)

    def hop_y(s, k):
        sy[s, k - 1] = acc[s, :, columns(lax.rem(y + k, NY) * HD, HD)].astype(BF16)
        arrive_y[s, k] = go(
            remote(sy.at[s, k - 1], ry.at[s, k - 1], sy_s.at[s, k - 1], ry_s.at[s, k - 1], dp, y_mate(k))
        )

    def send_y(s):
        for k in (2, 1, 3):
            arrive_x[s, k].wait_recv()
        acc[s] = acc[s] + rx[s, 0].astype(F32) + rx[s, 1].astype(F32) + rx[s, 2].astype(F32)
        for k in (2, 1, 3):
            hop_y(s, k)

    def send_x_heads(s, own):
        x_t[:, PLACE[s] * ROW : (PLACE[s] + 1) * ROW] = own
        flat = own.T
        for j in (3, 2, 1, 0):
            head = lax.rem(y + j, NY)
            for k in (2, 1, 3):
                at = columns((lax.rem(x + k, NX) * NY + head) * HD, HD)
                sh[j, k - 1] = jnp.dot(flat, w[:, at], preferred_element_type=F32).astype(BF16)
                arrive_x[s, j, k] = go(
                    remote(
                        sh.at[j, k - 1], rh.at[j, k - 1], hx_s.at[j, k - 1], hx_r.at[j, k - 1], dp, x_mate(k)
                    )
                )
        acc[s] = jnp.dot(flat, w[:, columns(x * GROUP, GROUP)], preferred_element_type=F32)

    def send_y_heads(s):
        for j in (3, 2, 1, 0):
            here = columns(lax.rem(y + j, NY) * HD, HD)
            for k in (2, 1, 3):
                arrive_x[s, j, k].wait_recv()
            acc[s, :, here] = (
                acc[s, :, here] + rh[j, 0].astype(F32) + rh[j, 1].astype(F32) + rh[j, 2].astype(F32)
            )
            if j:
                hop_y(s, j)

    def first(j, hh):
        return remote(offer.at[j], held.at[dp], first_s.at[hh, j], first_r.at[dp], dp_at(j, hh, j % 2), t)

    def second(j, d):
        return remote(picked.at[d], moved.at[j], second_s.at[d], second_r.at[j], d, t)

    def each_mid(act):
        for j in range(MIDS):
            for hh in (0, 1):

                @pl.when(dp != dp_at(j, hh, j % 2))
                def _(j=j, hh=hh):
                    act(j, hh)

    loads[0].wait()
    offer[...] = rows[jnp.clip(mine - 1, 0, CAP - 1)].reshape(MIDS, 2, 16, HD)

    @pl.when(is_mid)
    def _():
        pl.semaphore_wait(barrier, 12 + 2 * MIDS - 1 + column - 1)

    @pl.when(jnp.logical_not(is_mid))
    def _():
        pl.semaphore_wait(barrier, 12 + 2 * MIDS)

    each_mid(lambda j, hh: first(j, hh).start())

    loads[1].wait()
    send_x(0, jnp.where(0 < keep, rows[0], jnp.zeros((FEAT, ROW), BF16)))

    @pl.when(is_mid)
    def _():
        held[dp] = offer[z]

        @pl.loop(1, NDP)
        def _(k):
            s = lax.rem(dp + k, NDP)
            remote(offer.at[0], held.at[s], first_s.at[0, 0], first_r.at[s], dp, t).wait_recv()

        @pl.loop(1, column)
        def _(k):
            d = beside(k)
            picked[d] = held[partner[d]]
            second(z, d).start()

        moved[z] = held[partner[dp]]

    send_x(2, jnp.where(2 < keep, rows[2], jnp.zeros((FEAT, ROW), BF16)))

    is_key = t < KV
    gain = k_gain[...]
    gain_parts = []
    arrive_dy, arrive_dx, arrive_near, arrive_far = {}, {}, {}, {}

    def grads(s):
        return dkv_last if s == ORDER[-1] else dkv.at[PLACE[s] * ROW : (PLACE[s] + 1) * ROW]

    def norm(s):
        for k in (2, 1, 3):
            arrive_y[s, k].wait_recv()
        kv = acc[s, :, columns(y * HD, HD)] + ry[s, 0].astype(F32) + ry[s, 1].astype(F32) + ry[s, 2].astype(F32)
        live = s < new_count
        inverse = lax.rsqrt(jnp.mean(kv * kv, axis=-1, keepdims=True) + 1e-06)
        normed = kv * inverse
        g = jnp.where(live, cot[s].astype(F32), 0.0)
        gn = g * gain
        grad_key = inverse * (gn - normed * jnp.mean(gn * normed, axis=-1, keepdims=True))
        here = grads(s).at[:, columns(t * HD, HD)]
        here[...] = jnp.where(is_key, grad_key, g).astype(BF16)
        for k in (2, 3, 1):
            arrive_dy[s, k] = go(
                remote(here, here, day_s.at[s, k - 1], day_r.at[s, k - 1], dp, y_mate(k))
            )
        if s == ORDER[-1]:
            send_head(s, 0)
        kv_out[s] = jnp.where(live, jnp.where(is_key, normed * gain, kv), 0.0)
        gain_parts.append(jnp.sum((g * normed).reshape(ROW // 8, 8, HD), axis=0))

    def send_head(s, back):
        here = grads(s).at[:, columns((x * NY + lax.rem(y + NY - back, NY)) * HD, HD)]
        for k in (2, 1, 3):
            arrive_dx[back, k] = go(
                remote(here, here, hd_s.at[back, k - 1], hd_r.at[back, k - 1], dp, x_mate(k))
            )

    def group_rows(s, at, size, group):
        return (pl.ds(PLACE[s] * ROW + at, size), columns(lax.rem(group, NX) * GROUP, GROUP))

    def send_near(s):
        for k in (1, 3, 2):
            arrive_dy[s, k].wait_recv()
        here = group_rows(s, 0, ROW, x)
        for k in (1, 3):
            arrive_near[s, k] = go(
                remote(dkv.at[here], dkv.at[here], dax_s.at[s, k - 1], dax_r.at[s, k - 1], dp, x_mate(k))
            )

    def send_far(s):
        for n, k in enumerate((1, 3)):
            arrive_near[s, k].wait_recv()
            here = group_rows(s, 64 * n, 64, x + NX - k)
            arrive_far[s, k] = go(
                remote(dkv.at[here], dkv.at[here], dfx_s.at[s, n], dfx_r.at[s, n], dp, x_mate(k))
            )

    def row_grad(s):
        for k in (1, 3):
            if (s, k) in arrive_far:
                arrive_far[s, k].wait_recv()
        rg_out[s] = lax.dot_general(
            w[...], grads(s)[...], (((1,), (1,)), ((), ())), preferred_element_type=F32
        )

    send_y(0)
    send_y(2)
    loads[2].wait()
    norm(0)

    @pl.loop(0, MIDS)
    def _(j):
        @pl.when(dp != mid_at(j, yh))
        def _():
            second(j, dp).wait_recv()

    came = moved[...].reshape(FEAT, ROW)
    send_x_heads(1, jnp.where(1 < keep, rows[1], jnp.where(1 < new_count, came, jnp.zeros((FEAT, ROW), BF16))))
    norm(2)
    send_near(0)
    send_near(2)
    send_y_heads(1)
    send_far(0)
    send_far(2)
    norm(1)
    gain_all[t] = jnp.where(is_key, gain_parts[0] + gain_parts[1] + gain_parts[2], 0.0)
    arrive_gy, arrive_gx = {}, {}
    for k in (2, 1, 3):
        arrive_gy[k] = go(remote(gain_all.at[t], gain_all.at[t], gy_s.at[k - 1], gy_r.at[k - 1], dp, y_mate(k)))
    row_grad(0)
    for k in (1, 3, 2):
        arrive_dy[1, k].wait_recv()
        send_head(1, k)
    for k in (1, 3, 2):
        arrive_gy[k].wait_recv()
    for k in (2, 1, 3):
        here = pl.ds(x * NY, NY)
        arrive_gx[k] = go(remote(gain_all.at[here], gain_all.at[here], gx_s.at[k - 1], gx_r.at[k - 1], dp, x_mate(k)))
    row_grad(2)

    def product(half, buffer, rows_at, grad, add, each):
        for q in range(2):
            value = jnp.dot(
                x_t[:, rows_at], grad[:, columns(half * 1024 + q * GROUP, GROUP)], preferred_element_type=F32
            )
            for h in range(4):
                head = q * 4 + h
                for at, stop, to in segments(head):
                    lo, hi = (at - head * 20) * 16, (stop - head * 20) * 16
                    tiles = value[lo:hi, h * HD : (h + 1) * HD].reshape(stop - at, 16, HD)
                    buffer[to : to + stop - at] = buffer[to : to + stop - at] + tiles if add else tiles
            each(q)

    early, late = slice(0, 2 * ROW), slice(2 * ROW, 3 * ROW)
    product(1 - core, w_away, early, dkv, False, lambda q: None)
    product(core, w_own, early, dkv, False, lambda q: None)
    for k in (2, 1, 3):
        arrive_gx[k].wait_recv()
    gain_tile = jnp.concatenate([jnp.sum(gain_all[...], axis=0), jnp.zeros((8, HD), F32)], axis=0)
    for buffer in (w_away, w_own):
        for b in range(12):
            buffer[b * BLOCK + TILES] = gain_tile
        buffer[11 * BLOCK + 6 : 11 * BLOCK + TILES] = jnp.zeros((8, 16, HD), F32)
    for back in (0, 1, 3, 2):
        for k in (2, 1, 3):
            arrive_dx[back, k].wait_recv()

    cuts = ((0, 5 * BLOCK), (5 * BLOCK, 7 * BLOCK))
    arrive_core = []

    def send_half(q):
        at = pl.ds(*cuts[q])
        arrive_core.append(go(remote(w_away.at[at], w_core.at[at], core_s.at[q], core_r.at[q], mate, t)))

    product(1 - core, w_away, late, dkv_last, True, send_half)
    product(core, w_own, late, dkv_last, True, lambda q: None)
    for q in range(2):
        arrive_core[q].wait_recv()
        at = pl.ds(*cuts[q])
        w_own[at] = w_own[at] + w_core[at]

    def own_block(target, sub):
        return pl.ds(lax.rem(target + 2 * NZ, NZ) * BLOCK + sub[0], sub[1])

    ways = {
        -1: (ring_m, zm_s, zm_r, down, down_two),
        1: (ring_p, zp_s, zp_r, up, up_two),
    }
    arrive = {}

    def deep(sign, u):
        return (sign < 0) == (u == 0)

    def pass_on(sign, u, d):
        ring, send_sem, recv_sem, one, two = ways[sign]
        part = pl.ds(*SUBS[u])
        own = own_block(z + sign * d, SUBS[u])
        terms = {5: (6,) if deep(sign, u) else (), 3: (5, 4), 1: (3, 2)}.get(d, ())
        for n in terms:
            arrive[sign, u, n].wait_recv()
        if terms:
            value = w_own[own]
            for n in terms:
                value = value + ring[n - 1, part]
            src = ring.at[terms[0] - 1, part]
            src[...] = value
        else:
            src = w_own.at[own]
        to = two if d in (5, 3) else one
        arrive[sign, u, d] = go(
            remote(src, ring.at[d - 1, part], send_sem.at[d - 1, u], recv_sem.at[d - 1, u], to, t)
        )

    both = ((-1, 0), (1, 0), (-1, 1), (1, 1))
    flat_first = sorted(both, key=lambda way: (way[1], deep(*way)))
    for u in (0, 1):
        for sign in (-1, 1):
            pass_on(sign, u, 6 if deep(sign, u) else 5)
        for sign in (-1, 1):
            pass_on(sign, u, 4)
        if u == 0:
            for sign in (-1, 1):
                pass_on(sign, u, 2)
    row_grad(ORDER[-1])
    for way in both:
        if deep(*way):
            pass_on(*way, 5)
    for sign in (-1, 1):
        pass_on(sign, 1, 2)
    for way in flat_first:
        pass_on(*way, 3)
    for way in flat_first:
        pass_on(*way, 1)
    swaps = []
    for u, sub in enumerate(SUBS):
        part = pl.ds(*sub)
        for sign in (-1, 1):
            arrive[sign, u, 1].wait_recv()
        ring_m[0, part] = ring_m[0, part] + ring_p[0, part] + w_own[own_block(z, sub)]
        swaps.append(go(remote(ring_m.at[0, part], y_in.at[part], yh_s.at[u], yh_r.at[u], other_y, t)))
    live_rows = lax.fori_loop(0, NDP, lambda d, n: n + counts[d], 0)
    scale = lax.rsqrt(jnp.full((1, HD), live_rows * ROW, jnp.int32).astype(F32))
    ag = ag_out.at[core]

    def block(origin, u):
        return pl.ds(lax.rem(origin + 2 * NZ, NZ) * TILES + 7 * u, 7)

    spread, arrive_mate, seen = {}, [], set()

    def ready(sign, u, d):
        if (sign, u, d) not in seen:
            seen.add((sign, u, d))
            spread[sign, u, d].wait_recv()

    def hand_on(sign, u, d):
        back = (d - 1) // 2 * 2
        if back:
            ready(sign, u, back)
        at = block(z - sign * back, u)
        _, _, _, one, two = ways[sign]
        send_sem, recv_sem = (am_s, am_r) if sign < 0 else (ap_s, ap_r)
        spread[sign, u, d] = go(
            remote(ag.at[at], ag.at[at], send_sem.at[d - 1, u], recv_sem.at[d - 1, u], one if d % 2 else two, t)
        )

    def to_mate(origin):
        at = pl.ds(lax.rem(origin + 2 * NZ, NZ) * TILES, TILES)
        n = len(arrive_mate)
        arrive_mate.append(go(remote(ag.at[at], ag.at[at], mate_s.at[n], mate_r.at[n], mate, t)))

    def settle(d):
        for sign in (-1, 1):
            for u in (0, 1):
                ready(sign, u, d)
            to_mate(z - sign * d)

    for u, sub in enumerate(SUBS):
        swaps[u].wait_recv()
        at = pl.ds(sub[0], 7)
        ag_out[core, block(z, u)] = ((ring_m[0, at] + y_in[at]) * scale).astype(BF16)
        for d in (2, 1):
            for sign in (-1, 1):
                hand_on(sign, u, d)
    to_mate(z)
    gain_out[...] = jnp.sum(ring_m[0, TILES, :8, :] + y_in[TILES, :8, :], axis=0, keepdims=True) * scale
    for d in (4, 3):
        for way in both:
            hand_on(*way, d)
    settle(1)
    settle(2)
    for way in both:
        if deep(*way):
            hand_on(*way, 6)
    for way in both:
        hand_on(*way, 5)
    settle(3)
    settle(4)
    settle(5)
    for way in both:
        if deep(*way):
            ready(*way, 6)
    to_mate(z + 6)
    for copy in arrive_mate:
        copy.wait_recv()
    each_mid(lambda j, hh: first(j, hh).wait_send())

    @pl.when(is_mid)
    def _():
        @pl.loop(1, column)
        def _(k):
            second(z, beside(k)).wait_send()

    for copy in pending:
        copy.wait_send()


def finish_kernel(kv, rg, ag, gain, kv_out, rg_out, wg_out, gain_out):
    for h in range(4):
        wg_out[:, h * HD : (h + 1) * HD] = ag[0, h * 20 : h * 20 + 20].reshape(FEAT, HD).astype(F32)

    @pl.when(pl.program_id(0) == 0)
    def _():
        kv_out[...] = kv[...]
        rg_out[...] = rg[...]
        gain_out[...] = gain[...]


def main(counts, partner, rows, w, k_gain, cot):
    vmem = pl.BlockSpec(memory_space=pltpu.VMEM)
    smem = pl.BlockSpec(memory_space=pltpu.SMEM)
    hbm = pl.BlockSpec(memory_space=pl.ANY)
    dma = pltpu.SemaphoreType.DMA
    V = pltpu.VMEM
    kv, rg, ag, gain = pl.pallas_call(
        main_kernel,
        out_shape=(
            jax.ShapeDtypeStruct((BAL, ROW, HD), F32),
            jax.ShapeDtypeStruct((BAL, FEAT, ROW), F32),
            jax.ShapeDtypeStruct((2, NZ * TILES, 16, HD), BF16),
            jax.ShapeDtypeStruct((1, HD), F32),
        ),
        in_specs=[smem, smem, hbm, hbm, vmem, hbm],
        out_specs=(vmem,) * 4,
        scratch_shapes=[
            V((CAP, FEAT, ROW), BF16),
            V((FEAT, WIDE), BF16),
            V((BAL, ROW, HD), BF16),
            V((MIDS, 2, 16, HD), BF16),
            V((NDP, 2, 16, HD), BF16),
            V((NDP, 2, 16, HD), BF16),
            V((MIDS, 2, 16, HD), BF16),
            V((FEAT, BAL * ROW), BF16),
            V((BAL, 3, ROW, GROUP), BF16),
            V((BAL, 3, ROW, GROUP), BF16),
            V((BAL, ROW, GROUP), F32),
            V((BAL, 3, ROW, HD), BF16),
            V((BAL, 3, ROW, HD), BF16),
            V((2 * ROW, WIDE), BF16),
            V((ROW, WIDE), BF16),
            V((4, 3, ROW, HD), BF16),
            V((4, 3, ROW, HD), BF16),
            V((NX * NY, 8, HD), F32),
            V((NZ * BLOCK, 16, HD), F32),
            V((NZ * BLOCK, 16, HD), F32),
            V((NZ * BLOCK, 16, HD), F32),
            V((6, BLOCK, 16, HD), F32),
            V((6, BLOCK, 16, HD), F32),
            V((BLOCK, 16, HD), F32),
            dma((BAL, 3)), dma((BAL, 3)), dma((BAL, 3)), dma((BAL, 3)),
            dma((4, 3)), dma((4, 3)), dma((4, 3)), dma((4, 3)),
            dma((BAL, 3)), dma((BAL, 3)), dma((BAL, 3)), dma((BAL, 3)),
            dma((BAL, 2)), dma((BAL, 2)),
            dma((3,)), dma((3,)), dma((3,)), dma((3,)),
            dma((3,)), dma((2, MIDS)), dma((NDP,)), dma((NDP,)), dma((MIDS,)),
            dma((2,)), dma((2,)),
            dma((6, 2)), dma((6, 2)), dma((6, 2)), dma((6, 2)),
            dma((2,)), dma((2,)),
            dma((6, 2)), dma((6, 2)), dma((6, 2)), dma((6, 2)),
            dma((12,)), dma((12,)),
        ],
        compiler_params=pltpu.CompilerParams(
            collective_id=0, has_side_effects=True, vmem_limit_bytes=56 * 1024 * 1024
        ),
        name="kv_grads",
    )(counts, partner, rows, w, k_gain, cot)
    return pl.pallas_call(
        finish_kernel,
        grid=(4,),
        out_shape=(
            jax.ShapeDtypeStruct((BAL, ROW, HD), F32),
            jax.ShapeDtypeStruct((BAL, FEAT, ROW), F32),
            jax.ShapeDtypeStruct((FEAT, WIDE), F32),
            jax.ShapeDtypeStruct((1, HD), F32),
        ),
        in_specs=[
            pl.BlockSpec((BAL, ROW, HD), lambda i: (0, 0, 0)),
            pl.BlockSpec((BAL, FEAT, ROW), lambda i: (0, 0, 0)),
            pl.BlockSpec((1, HALF_TILES // 2, 16, HD), lambda i: (i // 2, i % 2, 0, 0)),
            pl.BlockSpec((1, HD), lambda i: (0, 0)),
        ],
        out_specs=(
            pl.BlockSpec((BAL, ROW, HD), lambda i: (0, 0, 0)),
            pl.BlockSpec((BAL, FEAT, ROW), lambda i: (0, 0, 0)),
            pl.BlockSpec((FEAT, GROUP), lambda i: (0, i)),
            pl.BlockSpec((1, HD), lambda i: (0, 0)),
        ),
        compiler_params=pltpu.CompilerParams(vmem_limit_bytes=56 * 1024 * 1024),
        name="unpack",
    )(kv, rg, ag, gain)


def shards(rows, counts, partner, w_kv, k_gain, cotangent):
    kv, rows_grad, weight_grad, gain_grad = main(
        counts, partner, jnp.swapaxes(rows, 1, 2), w_kv, k_gain.reshape(1, HD), cotangent
    )
    return kv, jnp.swapaxes(rows_grad, 1, 2), weight_grad, gain_grad.reshape(HD)


def solution(mesh):
    placed = (P("dp", None, "tensor"), P(), P(), P("tensor", None), P(), P("dp", None, "tensor"))
    return jax.shard_map(
        shards,
        mesh=mesh,
        in_specs=placed,
        out_specs=(P("dp", None, "tensor"), P("dp", None, "tensor"), P("tensor", None), P()),
        check_vma=False,
    )
```
